256 devices in a mesh: row: 8 (over x, z_hi), col: 32 (over z_lo, y, core).
Axes of the slice: x: 4, y: 4, z: 8 (z_hi: 2, z_lo: 4; z = z_hi * 4 + z_lo), core: 2. Of those that a mesh axis runs over, the one named last changes fastest.
Arguments:
- pair_state: bfloat16 [512, 512, 256], P('row', 'col'), may hold values from -6 to 6
- residue_mask: int32 [512], replicated, may hold values 0 or 1
- chain_ids: int32 [512], replicated, may hold values from 0 to 3, never falling along the last dimension, each value on 1 to 256 neighbouring positions
- gain_transition: float32 [256], replicated, may hold values from 0.1 to 1.9
- hidden_weight: bfloat16 [256, 1024], replicated, may hold values from -0.375 to 0.375
- out_weight: bfloat16 [1024, 256], replicated, may hold values from -0.1875 to 0.1875
- gain_attention: float32 [256], replicated, may hold values from 0.1 to 1.9
- query_weight: bfloat16 [256, 256], replicated, may hold values from -4 to 4
- key_weight: bfloat16 [256, 256], replicated, may hold values from -4 to 4
- value_weight: bfloat16 [256, 256], replicated, may hold values from -0.375 to 0.375
- gate_weight: bfloat16 [256, 256], replicated, may hold values from -0.375 to 0.375
- bias_weight: bfloat16 [256, 8], replicated, may hold values from -0.375 to 0.375
- chain_weight: float32 [8], replicated, may hold values from -2 to 2
- output_weight: bfloat16 [256, 256], replicated, may hold values from -4 to 4
Outputs:
- symmetric_pair: bfloat16 [512, 512, 256], P('row', 'col')
The draws below stay inside these ranges and needn't reach their ends.
All inputs are finite; a program needn't handle non-finite values.
Results may differ from the reference program's by a relative error of at most 0.004.
The reference program's roundings to bfloat16 on the way (of `first_norm`, `hidden_act`, `normed`, `pair_bias`, `attn_weights`, `gated` and `update`) count: a program that leaves them out, or rounds other values in their place, can miss the bound.
Values may be sent and summed in bfloat16 or wider, within the bound.
No kernel may reach another device: no remote copies, remote signals or barrier semaphores. Data moves between devices by JAX's collectives and lax.ppermute only.
A program may use at most 128 MiB of HBM per device.

```python
import math
import jax
import jax.numpy as jnp
import numpy as np
from jax import lax

PAIR_DIM = 256
HIDDEN_DIM = 1024
HEADS = 8
HEAD_DIM = 32
LENGTH = 512


def draw_query_weight(key, part):
    drawn = jax.random.normal(jax.random.fold_in(key, 21), (PAIR_DIM, HEADS * HEAD_DIM), jnp.float32) / math.sqrt(PAIR_DIM)
    return jnp.clip(drawn, -4.0, 4.0).astype(jnp.bfloat16)


def draw_key_weight(key, part):
    drawn = jax.random.normal(jax.random.fold_in(key, 23), (PAIR_DIM, HEADS * HEAD_DIM), jnp.float32) / math.sqrt(PAIR_DIM)
    return jnp.clip(drawn, -4.0, 4.0).astype(jnp.bfloat16)


def set_ends(values, stream_key, least, top_value):
    place = [jax.random.randint(jax.random.fold_in(stream_key, axis), (), 0, length) for axis, length in enumerate(values.shape)]
    longest = values.shape.index(max(values.shape))
    next_to = place[:longest] + [(place[longest] + 1) % values.shape[longest]] + place[longest + 1:]
    return values.at[tuple(place)].set(least).at[tuple(next_to)].set(top_value)


def block_levels(own_key, extent, shards, low, top_value):
    loudness, own = 1.0, jax.random.fold_in(own_key, 6)
    for dim, blocks in shards:
        heights = jnp.exp(jax.random.uniform(jax.random.fold_in(own, dim), (blocks,), jnp.float32, low / len(shards), top_value / len(shards)))
        loudness = loudness * jnp.repeat(heights, extent[dim] // blocks).reshape([-1 if axis == dim else 1 for axis in range(len(extent))])
    return loudness


def profile(amount, total, limit, lean):
    weights = [(1 << 20) // math.isqrt(rank ** lean) + 1 for rank in range(2, amount + 1)]
    spare, holding = total - limit - (amount - 1), [1] * (amount - 1)
    while spare > 0:
        candidates = [i for i in range(amount - 1) if holding[i] < limit]
        pool, budget = sum([weights[i] for i in candidates]), spare
        for i in candidates:
            extra = min(limit - holding[i], max(1, budget * weights[i] // pool), spare)
            holding[i] = holding[i] + extra
            spare = spare - extra
    return np.array([limit] + holding)


def uneven_parts(key, amount, total, bound, slope):
    if amount == 2:
        one = jax.random.randint(key, (), max(1, total - bound), min(bound, total - 1) + 1)
        return jnp.stack([one, total - one])
    tallies = jnp.asarray(profile(amount, total, bound, slope), jnp.int32)
    couples = (amount - 1) // 2
    source_of, receiver = tallies[1:1 + 2 * couples:2], tallies[2:2 + 2 * couples:2]
    slack = jnp.minimum(source_of - 1, bound - receiver)
    moved = jax.random.randint(jax.random.fold_in(key, 1), (couples,), 0, 1 << 20) % (slack + 1)
    tallies = tallies.at[1:1 + 2 * couples:2].set(source_of - moved).at[2:2 + 2 * couples:2].set(receiver + moved)
    return tallies[jax.random.permutation(jax.random.fold_in(key, 2), amount)]


def bell_draw(stream_key, extent, spread, reach, cuts=(), kind=jnp.bfloat16):
    entries = spread * jax.random.normal(stream_key, extent, jnp.float32)
    if cuts:
        entries = entries * block_levels(stream_key, extent, cuts, -0.22, 0.18)
    return jnp.clip(entries, -reach, reach).astype(kind)


def setup_inputs(seed: int = 0) -> dict:
    seeds = jax.random.split(jax.random.key(seed), 15)
    return {
        "pair_state": bell_draw(seeds[0], (LENGTH, LENGTH, PAIR_DIM), 1.0, 6.0, ((0, 8), (1, 32))),
        "residue_mask": set_ends((jax.random.randint(seeds[1], (LENGTH,), 0, 4) < 3).astype(jnp.int32), jax.random.fold_in(seeds[1], 1), 0, 1),
        "chain_ids": jnp.searchsorted(jnp.cumsum(uneven_parts(seeds[2], 4, LENGTH, LENGTH // 2, 0)), jnp.arange(LENGTH), side="right").astype(jnp.int32),
        "gain_transition": jnp.clip(1.0 + 0.18 * jax.random.normal(seeds[3], (PAIR_DIM,), jnp.float32), 0.1, 1.9),
        "hidden_weight": bell_draw(seeds[4], (PAIR_DIM, HIDDEN_DIM), PAIR_DIM ** -0.5, 0.375),
        "out_weight": bell_draw(seeds[5], (HIDDEN_DIM, PAIR_DIM), HIDDEN_DIM ** -0.5, 0.1875),
        "gain_attention": jnp.clip(1.0 + 0.18 * jax.random.normal(seeds[6], (PAIR_DIM,), jnp.float32), 0.1, 1.9),
        "query_weight": draw_query_weight(jax.random.fold_in(seeds[14], 71), 0),
        "key_weight": draw_key_weight(jax.random.fold_in(seeds[14], 71), 0),
        "value_weight": bell_draw(seeds[9], (PAIR_DIM, HEADS * HEAD_DIM), PAIR_DIM ** -0.5, 0.375),
        "gate_weight": bell_draw(seeds[10], (PAIR_DIM, HEADS * HEAD_DIM), PAIR_DIM ** -0.5, 0.375),
        "bias_weight": bell_draw(seeds[11], (PAIR_DIM, HEADS), PAIR_DIM ** -0.5, 0.375),
        "chain_weight": jnp.clip(jax.random.uniform(seeds[12], (HEADS,), jnp.float32, -2.0, 2.0), -2.0, 2.0),
        "output_weight": bell_draw(seeds[13], (HEADS * HEAD_DIM, PAIR_DIM), 0.25, 4.0),
    }


mask_penalty = 1000000000.0
norm_epsilon = 1e-05

def normalize(values, gain):
    center = values - lax.optimization_barrier(jnp.mean(values, axis=-1, keepdims=True))
    variance = lax.optimization_barrier(jnp.mean(center * center, axis=-1, keepdims=True))
    return center * lax.rsqrt(variance + norm_epsilon) * gain

def reference(pair_state, residue_mask, chain_ids, gain_transition, hidden_weight, out_weight, gain_attention, query_weight, key_weight, value_weight, gate_weight, bias_weight, chain_weight, output_weight):
    length = pair_state.shape[0]
    head_count = chain_weight.shape[0]
    head_dim = query_weight.shape[1] // head_count
    score_scale = 1.0 / math.sqrt(head_dim)
    positions = jnp.arange(length, dtype=jnp.int32)

    def transition_row(position):
        sym_row = pair_state[position].astype(jnp.float32) + pair_state[:, position].astype(jnp.float32)
        first_norm = normalize(sym_row, gain_transition).astype(jnp.bfloat16)
        hidden_act = jax.nn.relu(jnp.dot(first_norm, hidden_weight, preferred_element_type=jnp.float32)).astype(jnp.bfloat16)
        carried_row = sym_row + jnp.dot(hidden_act, out_weight, preferred_element_type=jnp.float32)
        normed_row = normalize(carried_row, gain_attention).astype(jnp.bfloat16)
        return (carried_row, normed_row)
    carried, normed = lax.map(transition_row, positions)

    def bias_row(normed_row):
        return jnp.dot(normed_row, bias_weight, preferred_element_type=jnp.float32).astype(jnp.bfloat16)
    pair_bias = jnp.transpose(lax.map(bias_row, normed), (2, 0, 1)).astype(jnp.float32)
    same_chain = (chain_ids[:, None] == chain_ids[None, :]).astype(jnp.float32)
    penalty = mask_penalty * (1 - residue_mask).astype(jnp.float32)
    full_bias = pair_bias + chain_weight[:, None, None] * same_chain[None] - penalty[None, None, :]

    def attend_row(normed_row):
        query_rows = jnp.dot(normed_row, query_weight, preferred_element_type=jnp.float32).astype(jnp.bfloat16).reshape(length, head_count, head_dim)
        key_rows = jnp.dot(normed_row, key_weight, preferred_element_type=jnp.float32).astype(jnp.bfloat16).reshape(length, head_count, head_dim)
        value_rows = jnp.dot(normed_row, value_weight, preferred_element_type=jnp.float32).astype(jnp.bfloat16).reshape(length, head_count, head_dim)
        gate_vals = jax.nn.sigmoid(jnp.dot(normed_row, gate_weight, preferred_element_type=jnp.float32))
        scores = jnp.einsum('jhd,khd->hjk', query_rows.astype(jnp.float32), key_rows.astype(jnp.float32)) * score_scale + full_bias
        row_max = lax.optimization_barrier(jnp.max(scores, axis=-1, keepdims=True))
        exponent = jnp.exp(scores - row_max)
        attn_weights = (exponent / lax.optimization_barrier(jnp.sum(exponent, axis=-1, keepdims=True))).astype(jnp.bfloat16)
        mixture = jnp.einsum('hjk,khd->jhd', attn_weights.astype(jnp.float32), value_rows.astype(jnp.float32)).reshape(length, head_count * head_dim)
        gated = (gate_vals * mixture).astype(jnp.bfloat16)
        return jnp.dot(gated, output_weight, preferred_element_type=jnp.float32).astype(jnp.bfloat16)
    update = lax.map(attend_row, normed)
    layer_out = carried + update.astype(jnp.float32)
    return (layer_out + jnp.swapaxes(layer_out, 0, 1)).astype(jnp.bfloat16)
```

```python
import math

import jax
import jax.numpy as jnp
from jax import lax
from jax.experimental import pallas as pl
from jax.experimental.pallas import tpu as pltpu
from jax.sharding import PartitionSpec as P

mask_penalty = 1000000000.0
norm_epsilon = 1e-05

X, ZH, ZL, Y, CORE = 4, 2, 4, 4, 2
ROWS, COLS = X * ZH, ZL * Y * CORE
RATIO = COLS // ROWS


def normalize(values, gain):
    center = values - jnp.mean(values, axis=-1, keepdims=True)
    variance = jnp.mean(center * center, axis=-1, keepdims=True)
    return center * lax.rsqrt(variance + norm_epsilon) * gain


def mirror_pairs(step):
    return [
        (r * COLS + c, (c // RATIO) * COLS + RATIO * r + (c + step) % RATIO)
        for r in range(ROWS)
        for c in range(COLS)
    ]


def shift_x(k):
    return [(r, ((r // ZH + k) % X) * ZH + r % ZH) for r in range(ROWS)]


def shift_zh(k):
    return [(r, (r // ZH) * ZH + (r + k) % ZH) for r in range(ROWS)]


def shift_zl(k):
    return [(c, (c + k * Y * CORE) % COLS) for c in range(COLS)]


def shift_y(k):
    return [
        (c, c - c % (Y * CORE) + (c + k * CORE) % (Y * CORE)) for c in range(COLS)
    ]


def shift_core(k):
    return [(c, c ^ k) for c in range(COLS)]


def gather_shifts(array, axis, pairs, count):
    return [array] + [lax.ppermute(array, axis, pairs(k)) for k in range(1, count)]


def in_order(pieces, me):
    count = len(pieces)
    twice = jnp.stack(pieces[::-1] + pieces[::-1])
    return lax.dynamic_slice_in_dim(twice, count - 1 - me, count, 0)


def transition_kernel(
    col_ref, own_ref, got0, got1, got2, got3, gain1_ref, w1_ref, w2_ref, gain2_ref, wb_ref,
    carried_ref, normed_ref, bias_ref,
):
    col = col_ref[0]
    tile_cols, tile_rows, channels = own_ref.shape
    width = tile_rows // RATIO
    for step, got in enumerate((got0, got1, got2, got3)):
        start = pl.multiple_of(lax.rem(col + RATIO - step, RATIO) * width, width)
        own = own_ref[:, pl.ds(start, width), :].astype(jnp.float32)
        sym = (own + got[...].astype(jnp.float32)).reshape(tile_cols * width, channels)
        first = normalize(sym, gain1_ref[...]).astype(jnp.bfloat16)
        hidden = jnp.maximum(
            jnp.dot(first, w1_ref[...], preferred_element_type=jnp.float32), 0.0
        ).astype(jnp.bfloat16)
        carried = sym + jnp.dot(hidden, w2_ref[...], preferred_element_type=jnp.float32)
        normed = normalize(carried, gain2_ref[...]).astype(jnp.bfloat16)
        carried_ref[:, pl.ds(start, width), :] = carried.reshape(tile_cols, width, channels)
        normed_ref[:, pl.ds(start, width), :] = normed.reshape(tile_cols, width, channels)
    for b in range(tile_cols):
        bias_ref[b] = lax.dot_general(
            wb_ref[...], normed_ref[b], (((1,), (1,)), ((), ())),
            preferred_element_type=jnp.float32,
        ).astype(jnp.bfloat16)


def transition(own, got, col, gain1, w1, w2, gain2, wb):
    tile_cols, tile_rows, channels = own.shape
    heads = wb.shape[1]
    vmem = pl.BlockSpec(memory_space=pltpu.VMEM)
    return pl.pallas_call(
        transition_kernel,
        out_shape=(
            jax.ShapeDtypeStruct(own.shape, jnp.float32),
            jax.ShapeDtypeStruct(own.shape, jnp.bfloat16),
            jax.ShapeDtypeStruct((tile_cols, heads, tile_rows), jnp.bfloat16),
        ),
        in_specs=[pl.BlockSpec(memory_space=pltpu.SMEM)] + [vmem] * 10,
        out_specs=(vmem, vmem, vmem),
        compiler_params=pltpu.CompilerParams(vmem_limit_bytes=40 << 20),
        name="transition",
    )(col, own, *got, gain1[None], w1, w2, gain2[None], wb.T)


def attention_kernel(
    place_ref, cw_ref, rows_ref, near_ref, far_ref, chain_col_ref, chain_row_ref, penalty_ref,
    wq_ref, wk_ref, wv_ref, wg_ref, wo_ref, out_ref, kt_ref, v_ref,
):
    zl = pl.program_id(0)
    my_y, my_core = place_ref[1], place_ref[2]
    parts, own_rows, part_len, channels = rows_ref.shape
    length = parts * part_len
    heads = near_ref.shape[2]
    head_dim = channels // heads
    scale = 1.0 / math.sqrt(head_dim)
    strip = near_ref.shape[3]

    @pl.when(zl == 0)
    def _():
        for i in range(own_rows):
            row = rows_ref[:, i].reshape(length, channels)
            kt_ref[i] = lax.dot_general(
                wk_ref[...], row, (((0,), (1,)), ((), ())), preferred_element_type=jnp.float32
            ).astype(jnp.bfloat16)
            v_ref[i] = jnp.dot(
                row, wv_ref[...], preferred_element_type=jnp.float32
            ).astype(jnp.bfloat16)

    places = []
    for core_step in range(CORE):
        for y_step in range(Y):
            y = lax.rem(my_y + Y - y_step, Y)
            core = lax.rem(my_core + core_step, CORE)
            within = y * CORE + core
            per_part = part_len // strip
            part = zl * (Y * CORE // per_part) + within // per_part
            start = pl.multiple_of(lax.rem(within, per_part) * strip, strip)
            places.append((part, start, pl.multiple_of(within * strip, strip)))
    block = len(places) * strip
    chain_rows = jnp.concatenate(
        [chain_col_ref[pl.ds(pl.multiple_of(zl * block, block) + w, strip), :] for _, _, w in places]
    )
    same = (chain_rows == chain_row_ref[...]).astype(jnp.float32)
    penalty = penalty_ref[...]
    lane_head = lax.broadcasted_iota(jnp.int32, (1, channels), 1) // head_dim
    queries, gates, mixes = [], [], []
    for i in range(own_rows):
        part_rows = jnp.concatenate(
            [rows_ref[part, i, pl.ds(start, strip), :] for part, start, _ in places]
        )
        queries.append(
            jnp.dot(part_rows, wq_ref[...], preferred_element_type=jnp.float32).astype(jnp.bfloat16)
        )
        gates.append(
            jax.nn.sigmoid(jnp.dot(part_rows, wg_ref[...], preferred_element_type=jnp.float32))
        )
        mixes.append(jnp.zeros((block, channels), jnp.float32))
    for h in range(heads):
        pair = jnp.concatenate(
            [near_ref[k, 0, h] for k in range(Y)] + [far_ref[k, 0, h] for k in range(Y)]
        ).astype(jnp.float32)
        full = pair + cw_ref[h] * same - penalty
        mine = lane_head == h
        for i in range(own_rows):
            query = jnp.where(mine, queries[i], jnp.zeros_like(queries[i]))
            scores = (
                jnp.dot(query, kt_ref[i], preferred_element_type=jnp.float32) * scale + full
            )
            exponent = jnp.exp(scores - jnp.max(scores, axis=-1, keepdims=True))
            weights = (
                exponent * (1.0 / jnp.sum(exponent, axis=-1, keepdims=True))
            ).astype(jnp.bfloat16)
            mix = jnp.dot(weights, v_ref[i], preferred_element_type=jnp.float32)
            mixes[i] = jnp.where(mine, mix, mixes[i])
    for i in range(own_rows):
        gated = (gates[i] * mixes[i]).astype(jnp.bfloat16)
        update = jnp.dot(gated, wo_ref[...], preferred_element_type=jnp.float32).astype(
            jnp.bfloat16
        )
        for n, (part, start, _) in enumerate(places):
            out_ref[part, i, pl.ds(start, strip), :] = update[n * strip : (n + 1) * strip]


def attention(rows, near, far, place, chain_weight, chain_ids, penalty, wq, wk, wv, wg, wo):
    parts, own_rows, part_len, channels = rows.shape
    length = parts * part_len
    heads, strip = near.shape[2], near.shape[3]
    smem = pl.BlockSpec(memory_space=pltpu.SMEM)

    def whole(shape):
        return pl.BlockSpec(shape, lambda z, place: (0,) * len(shape))

    strips = pl.BlockSpec(
        (Y, 1, heads, strip, length),
        lambda z, place: (0, lax.rem(place[0] + ZL - z, ZL), 0, 0, 0),
    )
    weight = whole((channels, channels))
    return pl.pallas_call(
        attention_kernel,
        out_shape=jax.ShapeDtypeStruct(rows.shape, jnp.bfloat16),
        grid_spec=pltpu.PrefetchScalarGridSpec(
            num_scalar_prefetch=1,
            grid=(ZL,),
            in_specs=[
                smem, whole(rows.shape), strips, strips,
                whole((length, 1)), whole((1, length)), whole((1, length)),
                weight, weight, weight, weight, weight,
            ],
            out_specs=whole(rows.shape),
            scratch_shapes=[
                pltpu.VMEM((own_rows, channels, length), jnp.bfloat16),
                pltpu.VMEM((own_rows, length, channels), jnp.bfloat16),
            ],
        ),
        compiler_params=pltpu.CompilerParams(vmem_limit_bytes=48 << 20),
        name="attention",
    )(
        place, chain_weight, rows, near, far, chain_ids[:, None], chain_ids[None, :],
        penalty[None, :], wq, wk, wv, wg, wo,
    )


def per_device(
    pair_state,
    residue_mask,
    chain_ids,
    gain_transition,
    hidden_weight,
    out_weight,
    gain_attention,
    query_weight,
    key_weight,
    value_weight,
    gate_weight,
    bias_weight,
    chain_weight,
    output_weight,
):
    tile_rows, tile_cols, channels = pair_state.shape
    heads = chain_weight.shape[0]
    row, col = lax.axis_index("row"), lax.axis_index("col")
    my_zl, my_y, my_core = col // (Y * CORE), col // CORE % Y, col % CORE

    blocks = pair_state.reshape(RATIO, tile_cols, tile_cols, channels)
    got = []
    for step in range(RATIO):
        piece = lax.dynamic_index_in_dim(blocks, (col + step) % RATIO, 0, keepdims=False)
        got.append(lax.ppermute(piece, ("row", "col"), mirror_pairs(step)))
    own = jnp.transpose(pair_state, (1, 0, 2))
    carried, normed, bias = transition(
        own, got, col.reshape(1), gain_transition, hidden_weight, out_weight, gain_attention,
        bias_weight,
    )

    sent = normed.reshape(ROWS, tile_cols // ROWS, tile_rows, channels)
    rows = jnp.transpose(sent, (0, 1, 2, 3))
    rows = lax.all_to_all(rows, "row", split_axis=0, concat_axis=0, tiled=True)

    by_x = in_order(gather_shifts(bias, "row", shift_x, X), row // ZH)
    by_zh = in_order(gather_shifts(by_x, "row", shift_zh, ZH), row % ZH)
    strip = jnp.transpose(by_zh, (3, 2, 1, 0, 4)).reshape(heads, tile_cols, ROWS * tile_rows)
    by_zl = jnp.stack(gather_shifts(strip, "col", shift_zl, ZL))
    near = jnp.stack(gather_shifts(by_zl, "col", shift_y, Y))
    far = lax.ppermute(near, "col", shift_core(1))

    penalty = mask_penalty * (1 - residue_mask).astype(jnp.float32)
    place = jnp.stack([my_zl, my_y, my_core]).astype(jnp.int32)
    update = attention(
        rows, near, far, place, chain_weight, chain_ids, penalty,
        query_weight, key_weight, value_weight, gate_weight, output_weight,
    )
    back = lax.all_to_all(update, "row", split_axis=0, concat_axis=0, tiled=True).reshape(
        tile_cols, tile_rows, channels
    )
    other = []
    for step in range(RATIO):
        start = (col + step) % RATIO * tile_cols
        piece = lax.dynamic_slice_in_dim(back, start, tile_cols, 1)
        other.append(lax.ppermute(piece, ("row", "col"), mirror_pairs(step)))
    base = jnp.transpose(2.0 * carried + back.astype(jnp.float32), (1, 0, 2))
    other = in_order(other, col % RATIO).reshape(tile_rows, tile_cols, channels)
    return (base + other.astype(jnp.float32)).astype(jnp.bfloat16)


def solution(mesh):
    placed = (P("row", "col", None),) + (P(),) * 13
    return jax.shard_map(
        per_device, mesh=mesh, in_specs=placed, out_specs=P("row", "col", None), check_vma=False
    )
```

```python
import math

import jax
import jax.numpy as jnp
from jax import lax
from jax.experimental import pallas as pl
from jax.experimental.pallas import tpu as pltpu
from jax.sharding import PartitionSpec as P

mask_penalty = 1000000000.0
norm_epsilon = 1e-05

X, ZH, ZL, Y, CORE = 4, 2, 4, 4, 2
ROWS, COLS = X * ZH, ZL * Y * CORE
RATIO = COLS // ROWS


def normalize(values, gain):
    center = values - jnp.mean(values, axis=-1, keepdims=True)
    variance = jnp.mean(center * center, axis=-1, keepdims=True)
    return center * lax.rsqrt(variance + norm_epsilon) * gain


def place_of(device):
    row, col = divmod(device, COLS)
    return row // ZH, row % ZH, col // (Y * CORE), col // CORE % Y, col % CORE


def device_of(x, zh, zl, y, core):
    return (x * ZH + zh) * COLS + (zl * Y + y) * CORE + core


def via(device, block, back=1):
    x, zh, zl, y, core = place_of(device)
    y_step = Y // 2 * (block % 2)
    return device_of((x + back * block) % X, zh, zl, (y + back * y_step) % Y, core)


def out_pairs(block):
    return [(d, via(d, block)) for d in range(ROWS * COLS)]


def mirror_pairs(step):
    pairs = []
    for d in range(ROWS * COLS):
        block = (d + step) % RATIO
        row, col = divmod(via(d, block, -1), COLS)
        pairs.append((d, (col // RATIO) * COLS + RATIO * row + block))
    return pairs


def to_mirror(blocks, col):
    both = ("row", "col")
    held = jnp.stack(
        [blocks[0]] + [lax.ppermute(blocks[m], both, out_pairs(m)) for m in range(1, RATIO)]
    )
    return [
        lax.ppermute(
            lax.dynamic_index_in_dim(held, (col + step) % RATIO, 0, keepdims=False),
            both,
            mirror_pairs(step),
        )
        for step in range(RATIO)
    ]


def shift_x(k):
    return [(r, ((r // ZH + k) % X) * ZH + r % ZH) for r in range(ROWS)]


def shift_zh(k):
    return [(r, (r // ZH) * ZH + (r + k) % ZH) for r in range(ROWS)]


def shift_zl(k):
    return [(c, (c + k * Y * CORE) % COLS) for c in range(COLS)]


def shift_y(k):
    return [
        (c, c - c % (Y * CORE) + (c + k * CORE) % (Y * CORE)) for c in range(COLS)
    ]


def shift_core(k):
    return [(c, c ^ k) for c in range(COLS)]


def gather_shifts(array, axis, pairs, count):
    return [array] + [lax.ppermute(array, axis, pairs(k)) for k in range(1, count)]


def in_order(pieces, me):
    count = len(pieces)
    twice = jnp.stack(pieces[::-1] + pieces[::-1])
    return lax.dynamic_slice_in_dim(twice, count - 1 - me, count, 0)


def transition_kernel(
    col_ref, own_ref, got0, got1, got2, got3, gain1_ref, w1_ref, w2_ref, gain2_ref, wb_ref,
    carried_ref, normed_ref, bias_ref,
):
    col = col_ref[0]
    tile_cols, tile_rows, channels = own_ref.shape
    width = tile_rows // RATIO
    for step, got in enumerate((got0, got1, got2, got3)):
        start = pl.multiple_of(lax.rem(col + RATIO - step, RATIO) * width, width)
        own = own_ref[:, pl.ds(start, width), :].astype(jnp.float32)
        sym = (own + got[...].astype(jnp.float32)).reshape(tile_cols * width, channels)
        first = normalize(sym, gain1_ref[...]).astype(jnp.bfloat16)
        hidden = jnp.maximum(
            jnp.dot(first, w1_ref[...], preferred_element_type=jnp.float32), 0.0
        ).astype(jnp.bfloat16)
        carried = sym + jnp.dot(hidden, w2_ref[...], preferred_element_type=jnp.float32)
        normed = normalize(carried, gain2_ref[...]).astype(jnp.bfloat16)
        carried_ref[:, pl.ds(start, width), :] = carried.reshape(tile_cols, width, channels)
        normed_ref[:, pl.ds(start, width), :] = normed.reshape(tile_cols, width, channels)
    for b in range(tile_cols):
        bias_ref[b] = lax.dot_general(
            wb_ref[...], normed_ref[b], (((1,), (1,)), ((), ())),
            preferred_element_type=jnp.float32,
        ).astype(jnp.bfloat16)


def transition(own, got, col, gain1, w1, w2, gain2, wb):
    tile_cols, tile_rows, channels = own.shape
    heads = wb.shape[1]
    vmem = pl.BlockSpec(memory_space=pltpu.VMEM)
    return pl.pallas_call(
        transition_kernel,
        out_shape=(
            jax.ShapeDtypeStruct(own.shape, jnp.float32),
            jax.ShapeDtypeStruct(own.shape, jnp.bfloat16),
            jax.ShapeDtypeStruct((tile_cols, heads, tile_rows), jnp.bfloat16),
        ),
        in_specs=[pl.BlockSpec(memory_space=pltpu.SMEM)] + [vmem] * 10,
        out_specs=(vmem, vmem, vmem),
        compiler_params=pltpu.CompilerParams(vmem_limit_bytes=40 << 20),
        name="transition",
    )(col, own, *got, gain1[None], w1, w2, gain2[None], wb.T)


def attention_kernel(
    place_ref, cw_ref, rows_ref, near_ref, far_ref, chain_col_ref, chain_row_ref, penalty_ref,
    wq_ref, wk_ref, wv_ref, wg_ref, wo_ref, out_ref, kt_ref, v_ref,
):
    zl = pl.program_id(0)
    my_y, my_core = place_ref[1], place_ref[2]
    parts, own_rows, part_len, channels = rows_ref.shape
    length = parts * part_len
    heads = near_ref.shape[2]
    head_dim = channels // heads
    scale = 1.0 / math.sqrt(head_dim)
    strip = near_ref.shape[3]

    @pl.when(zl == 0)
    def _():
        for i in range(own_rows):
            row = rows_ref[:, i].reshape(length, channels)
            kt_ref[i] = lax.dot_general(
                wk_ref[...], row, (((0,), (1,)), ((), ())), preferred_element_type=jnp.float32
            ).astype(jnp.bfloat16)
            v_ref[i] = jnp.dot(
                row, wv_ref[...], preferred_element_type=jnp.float32
            ).astype(jnp.bfloat16)

    places = []
    for core_step in range(CORE):
        for y_step in range(Y):
            y = lax.rem(my_y + Y - y_step, Y)
            core = lax.rem(my_core + core_step, CORE)
            within = y * CORE + core
            per_part = part_len // strip
            part = zl * (Y * CORE // per_part) + within // per_part
            start = pl.multiple_of(lax.rem(within, per_part) * strip, strip)
            places.append((part, start, pl.multiple_of(within * strip, strip)))
    block = len(places) * strip
    chain_rows = jnp.concatenate(
        [chain_col_ref[pl.ds(pl.multiple_of(zl * block, block) + w, strip), :] for _, _, w in places]
    )
    same = (chain_rows == chain_row_ref[...]).astype(jnp.float32)
    penalty = penalty_ref[...]
    lane_head = lax.broadcasted_iota(jnp.int32, (1, channels), 1) // head_dim
    queries, gates, mixes = [], [], []
    for i in range(own_rows):
        part_rows = jnp.concatenate(
            [rows_ref[part, i, pl.ds(start, strip), :] for part, start, _ in places]
        )
        queries.append(
            jnp.dot(part_rows, wq_ref[...], preferred_element_type=jnp.float32).astype(jnp.bfloat16)
        )
        gates.append(
            jax.nn.sigmoid(jnp.dot(part_rows, wg_ref[...], preferred_element_type=jnp.float32))
        )
        mixes.append(jnp.zeros((block, channels), jnp.float32))
    for h in range(heads):
        pair = jnp.concatenate(
            [near_ref[k, 0, h] for k in range(Y)] + [far_ref[k, 0, h] for k in range(Y)]
        ).astype(jnp.float32)
        full = pair + cw_ref[h] * same - penalty
        mine = lane_head == h
        for i in range(own_rows):
            query = jnp.where(mine, queries[i], jnp.zeros_like(queries[i]))
            scores = (
                jnp.dot(query, kt_ref[i], preferred_element_type=jnp.float32) * scale + full
            )
            exponent = jnp.exp(scores - jnp.max(scores, axis=-1, keepdims=True))
            weights = (
                exponent * (1.0 / jnp.sum(exponent, axis=-1, keepdims=True))
            ).astype(jnp.bfloat16)
            mix = jnp.dot(weights, v_ref[i], preferred_element_type=jnp.float32)
            mixes[i] = jnp.where(mine, mix, mixes[i])
    for i in range(own_rows):
        gated = (gates[i] * mixes[i]).astype(jnp.bfloat16)
        update = jnp.dot(gated, wo_ref[...], preferred_element_type=jnp.float32).astype(
            jnp.bfloat16
        )
        for n, (part, start, _) in enumerate(places):
            out_ref[part, i, pl.ds(start, strip), :] = update[n * strip : (n + 1) * strip]


def attention(rows, near, far, place, chain_weight, chain_ids, penalty, wq, wk, wv, wg, wo):
    parts, own_rows, part_len, channels = rows.shape
    length = parts * part_len
    heads, strip = near.shape[2], near.shape[3]
    smem = pl.BlockSpec(memory_space=pltpu.SMEM)

    def whole(shape):
        return pl.BlockSpec(shape, lambda z, place: (0,) * len(shape))

    strips = pl.BlockSpec(
        (Y, 1, heads, strip, length),
        lambda z, place: (0, lax.rem(place[0] + ZL - z, ZL), 0, 0, 0),
    )
    weight = whole((channels, channels))
    return pl.pallas_call(
        attention_kernel,
        out_shape=jax.ShapeDtypeStruct(rows.shape, jnp.bfloat16),
        grid_spec=pltpu.PrefetchScalarGridSpec(
            num_scalar_prefetch=1,
            grid=(ZL,),
            in_specs=[
                smem, whole(rows.shape), strips, strips,
                whole((length, 1)), whole((1, length)), whole((1, length)),
                weight, weight, weight, weight, weight,
            ],
            out_specs=whole(rows.shape),
            scratch_shapes=[
                pltpu.VMEM((own_rows, channels, length), jnp.bfloat16),
                pltpu.VMEM((own_rows, length, channels), jnp.bfloat16),
            ],
        ),
        compiler_params=pltpu.CompilerParams(vmem_limit_bytes=48 << 20),
        name="attention",
    )(
        place, chain_weight, rows, near, far, chain_ids[:, None], chain_ids[None, :],
        penalty[None, :], wq, wk, wv, wg, wo,
    )


def per_device(
    pair_state,
    residue_mask,
    chain_ids,
    gain_transition,
    hidden_weight,
    out_weight,
    gain_attention,
    query_weight,
    key_weight,
    value_weight,
    gate_weight,
    bias_weight,
    chain_weight,
    output_weight,
):
    tile_rows, tile_cols, channels = pair_state.shape
    heads = chain_weight.shape[0]
    row, col = lax.axis_index("row"), lax.axis_index("col")
    my_zl, my_y, my_core = col // (Y * CORE), col // CORE % Y, col % CORE

    blocks = pair_state.reshape(RATIO, tile_cols, tile_cols, channels)
    got = to_mirror(blocks, col)
    own = jnp.transpose(pair_state, (1, 0, 2))
    carried, normed, bias = transition(
        own, got, col.reshape(1), gain_transition, hidden_weight, out_weight, gain_attention,
        bias_weight,
    )

    sent = normed.reshape(ROWS, tile_cols // ROWS, tile_rows, channels)
    rows = lax.all_to_all(sent, "row", split_axis=0, concat_axis=0, tiled=True)

    by_x = in_order(gather_shifts(bias, "row", shift_x, X), row // ZH)
    by_zh = in_order(gather_shifts(by_x, "row", shift_zh, ZH), row % ZH)
    strip = jnp.transpose(by_zh, (3, 2, 1, 0, 4)).reshape(heads, tile_cols, ROWS * tile_rows)
    strip, rows = lax.optimization_barrier((strip, rows))
    by_zl = jnp.stack(gather_shifts(strip, "col", shift_zl, ZL))
    near = jnp.stack(gather_shifts(by_zl, "col", shift_y, Y))
    far = lax.ppermute(near, "col", shift_core(1))

    penalty = mask_penalty * (1 - residue_mask).astype(jnp.float32)
    place = jnp.stack([my_zl, my_y, my_core]).astype(jnp.int32)
    update = attention(
        rows, near, far, place, chain_weight, chain_ids, penalty,
        query_weight, key_weight, value_weight, gate_weight, output_weight,
    )
    back = lax.all_to_all(update, "row", split_axis=0, concat_axis=0, tiled=True).reshape(
        tile_cols, tile_rows, channels
    )
    blocks = [back[:, m * tile_cols : (m + 1) * tile_cols] for m in range(RATIO)]
    other = to_mirror(blocks, col)
    base = jnp.transpose(2.0 * carried + back.astype(jnp.float32), (1, 0, 2))
    other = in_order(other, col % RATIO).reshape(tile_rows, tile_cols, channels)
    return (base + other.astype(jnp.float32)).astype(jnp.bfloat16)


def solution(mesh):
    placed = (P("row", "col", None),) + (P(),) * 13
    return jax.shard_map(
        per_device, mesh=mesh, in_specs=placed, out_specs=P("row", "col", None), check_vma=False
    )
```

```python
import math

import jax
import jax.numpy as jnp
from jax import lax
from jax.experimental import pallas as pl
from jax.experimental.pallas import tpu as pltpu
from jax.sharding import PartitionSpec as P

mask_penalty = 1000000000.0
norm_epsilon = 1e-05

X, ZH, ZL, Y, CORE = 4, 2, 4, 4, 2
ROWS, COLS = X * ZH, ZL * Y * CORE
RATIO = COLS // ROWS


def normalize(values, gain):
    center = values - jnp.mean(values, axis=-1, keepdims=True)
    variance = jnp.mean(center * center, axis=-1, keepdims=True)
    return center * lax.rsqrt(variance + norm_epsilon) * gain


def place_of(device):
    row, col = divmod(device, COLS)
    return row // ZH, row % ZH, col // (Y * CORE), col // CORE % Y, col % CORE


def device_of(x, zh, zl, y, core):
    return (x * ZH + zh) * COLS + (zl * Y + y) * CORE + core


def via(device, block, back=1, y_step=Y // 2):
    x, zh, zl, y, core = place_of(device)
    return device_of(
        (x + back * block) % X, zh, zl, (y + back * y_step * (block % 2)) % Y, core
    )


def out_pairs(block):
    return [(d, via(d, block)) for d in range(ROWS * COLS)]


def mirror_pairs(step, y_step):
    pairs = []
    for d in range(ROWS * COLS):
        block = (d + step) % RATIO
        row, col = divmod(via(d, block, -1, y_step), COLS)
        pairs.append((d, (col // RATIO) * COLS + RATIO * row + block))
    return pairs


def spread(blocks):
    return [blocks[0]] + [
        lax.ppermute(blocks[m], ("row", "col"), out_pairs(m)) for m in range(1, RATIO)
    ]


def to_mirror(held, col, y_step):
    return [
        lax.ppermute(
            lax.dynamic_index_in_dim(held, (col + step) % RATIO, 0, keepdims=False),
            ("row", "col"),
            mirror_pairs(step, y_step),
        )
        for step in range(RATIO)
    ]


def shift_x(k):
    return [(r, ((r // ZH + k) % X) * ZH + r % ZH) for r in range(ROWS)]


def shift_zh(k):
    return [(r, (r // ZH) * ZH + (r + k) % ZH) for r in range(ROWS)]


def shift_zl(k):
    return [(c, (c + k * Y * CORE) % COLS) for c in range(COLS)]


def shift_y(k):
    return [
        (c, c - c % (Y * CORE) + (c + k * CORE) % (Y * CORE)) for c in range(COLS)
    ]


def shift_core(k):
    return [(c, c ^ k) for c in range(COLS)]


def gather_shifts(array, axis, pairs, count):
    return [array] + [lax.ppermute(array, axis, pairs(k)) for k in range(1, count)]


def in_order(pieces, me):
    count = len(pieces)
    twice = jnp.stack(pieces[::-1] + pieces[::-1])
    return lax.dynamic_slice_in_dim(twice, count - 1 - me, count, 0)


def transition_kernel(
    col_ref, own_ref, got0, got1, got2, got3, gain1_ref, w1_ref, w2_ref, gain2_ref, wb_ref,
    carried_ref, normed_ref, bias_ref,
):
    col = col_ref[0]
    tile_cols, tile_rows, channels = own_ref.shape
    width = tile_rows // RATIO
    for step, got in enumerate((got0, got1, got2, got3)):
        start = pl.multiple_of(lax.rem(col + RATIO - step, RATIO) * width, width)
        own = own_ref[:, pl.ds(start, width), :].astype(jnp.float32)
        sym = (own + got[...].astype(jnp.float32)).reshape(tile_cols * width, channels)
        first = normalize(sym, gain1_ref[...]).astype(jnp.bfloat16)
        hidden = jnp.maximum(
            jnp.dot(first, w1_ref[...], preferred_element_type=jnp.float32), 0.0
        ).astype(jnp.bfloat16)
        carried = sym + jnp.dot(hidden, w2_ref[...], preferred_element_type=jnp.float32)
        normed = normalize(carried, gain2_ref[...]).astype(jnp.bfloat16)
        carried_ref[:, pl.ds(start, width), :] = carried.reshape(tile_cols, width, channels)
        normed_ref[:, pl.ds(start, width), :] = normed.reshape(tile_cols, width, channels)
    for b in range(tile_cols):
        bias_ref[b] = lax.dot_general(
            wb_ref[...], normed_ref[b], (((1,), (1,)), ((), ())),
            preferred_element_type=jnp.float32,
        ).astype(jnp.bfloat16)


def transition(own, got, col, gain1, w1, w2, gain2, wb):
    tile_cols, tile_rows, channels = own.shape
    heads = wb.shape[1]
    vmem = pl.BlockSpec(memory_space=pltpu.VMEM)
    return pl.pallas_call(
        transition_kernel,
        out_shape=(
            jax.ShapeDtypeStruct(own.shape, jnp.float32),
            jax.ShapeDtypeStruct(own.shape, jnp.bfloat16),
            jax.ShapeDtypeStruct((tile_cols, heads, tile_rows), jnp.bfloat16),
        ),
        in_specs=[pl.BlockSpec(memory_space=pltpu.SMEM)] + [vmem] * 10,
        out_specs=(vmem, vmem, vmem),
        compiler_params=pltpu.CompilerParams(vmem_limit_bytes=40 << 20),
        name="transition",
    )(col, own, *got, gain1[None], w1, w2, gain2[None], wb.T)


def attention_kernel(
    place_ref, cw_ref, rows_ref, near_a_ref, far_a_ref, near_b_ref, far_b_ref, chain_col_ref,
    chain_row_ref, penalty_ref, wq_ref, wk_ref, wv_ref, wg_ref, wo_ref, out_ref, kt_ref, v_ref,
):
    zl = pl.program_id(0)
    my_x, my_y, my_core = place_ref[0], place_ref[2], place_ref[3]
    parts, own_rows, part_len, channels = rows_ref.shape
    half, strip = near_a_ref.shape[3], near_a_ref.shape[4]
    heads = 2 * half
    head_dim = channels // heads
    scale = 1.0 / math.sqrt(head_dim)
    xs = [lax.rem(my_x + X - step, X) for step in range(X)]

    @pl.when(zl == 0)
    def _():
        for i in range(own_rows):
            row = jnp.concatenate(
                [rows_ref[x * ZH + zh, i] for x in xs for zh in range(ZH)]
            )
            kt_ref[i] = lax.dot_general(
                wk_ref[...], row, (((0,), (1,)), ((), ())), preferred_element_type=jnp.float32
            ).astype(jnp.bfloat16)
            v_ref[i] = jnp.dot(
                row, wv_ref[...], preferred_element_type=jnp.float32
            ).astype(jnp.bfloat16)

    per_part = part_len // strip
    places = []
    for core_step in range(CORE):
        for y_step in range(Y):
            y = lax.rem(my_y + Y - y_step, Y)
            core = lax.rem(my_core + core_step, CORE)
            within = y * CORE + core
            part = zl * (Y * CORE // per_part) + within // per_part
            block = lax.rem(within, per_part)
            places.append((part, block, pl.multiple_of(within * strip, strip)))
    rows_here = len(places) * strip
    first = pl.multiple_of(zl * rows_here, rows_here)
    chain_rows = jnp.concatenate(
        [chain_col_ref[pl.ds(first + w, strip), :] for _, _, w in places]
    )
    chain_keys = jnp.concatenate([chain_row_ref[pl.ds(x, 1), :] for x in xs], axis=1)
    penalty = jnp.concatenate([penalty_ref[pl.ds(x, 1), :] for x in xs], axis=1)
    same = (chain_rows == chain_keys).astype(jnp.float32)
    lane_head = lax.broadcasted_iota(jnp.int32, (1, channels), 1) // head_dim
    queries, gates, mixes = [], [], []
    for i in range(own_rows):
        part_rows = jnp.concatenate(
            [
                rows_ref[part, i, pl.ds(pl.multiple_of(block * strip, strip), strip), :]
                for part, block, _ in places
            ]
        )
        queries.append(
            jnp.dot(part_rows, wq_ref[...], preferred_element_type=jnp.float32).astype(jnp.bfloat16)
        )
        gates.append(
            jax.nn.sigmoid(jnp.dot(part_rows, wg_ref[...], preferred_element_type=jnp.float32))
        )
        mixes.append(jnp.zeros((rows_here, channels), jnp.float32))
    for h in range(heads):
        strips = []
        for a_ref, b_ref in ((near_a_ref, near_b_ref), (far_a_ref, far_b_ref)):
            for y_step in range(Y):
                if h < half:
                    chunks = [a_ref[y_step, 0, k, h] for k in range(X)]
                else:
                    chunks = [b_ref[k, y_step, 0, h - half] for k in range(X)]
                strips.append(jnp.concatenate(chunks, axis=1))
        pair = jnp.concatenate(strips).astype(jnp.float32)
        full = pair + cw_ref[h] * same - penalty
        mine = lane_head == h
        for i in range(own_rows):
            query = jnp.where(mine, queries[i], jnp.zeros_like(queries[i]))
            scores = (
                jnp.dot(query, kt_ref[i], preferred_element_type=jnp.float32) * scale + full
            )
            exponent = jnp.exp(scores - jnp.max(scores, axis=-1, keepdims=True))
            weights = (
                exponent * (1.0 / jnp.sum(exponent, axis=-1, keepdims=True))
            ).astype(jnp.bfloat16)
            mix = jnp.dot(weights, v_ref[i], preferred_element_type=jnp.float32)
            mixes[i] = jnp.where(mine, mix, mixes[i])
    for i in range(own_rows):
        gated = (gates[i] * mixes[i]).astype(jnp.bfloat16)
        update = jnp.dot(gated, wo_ref[...], preferred_element_type=jnp.float32).astype(
            jnp.bfloat16
        )
        for n, (part, block, _) in enumerate(places):
            to = lax.rem(part // ZH + block, X) * ZH + lax.rem(part, ZH)
            out_ref[to, i, block] = update[n * strip : (n + 1) * strip]


def attention(rows, near, far, place, chain_weight, chain_ids, penalty, wq, wk, wv, wg, wo):
    parts, own_rows, part_len, channels = rows.shape
    half, strip, width = near.shape[3:]
    length = parts * part_len
    smem = pl.BlockSpec(memory_space=pltpu.SMEM)

    def whole(shape):
        return pl.BlockSpec(shape, lambda z, place: (0,) * len(shape))

    first = pl.BlockSpec(
        (Y, 1, X, half, strip, width),
        lambda z, place: (0, lax.rem(place[1] + ZL - z, ZL), 0, 0, 0, 0),
    )
    second = pl.BlockSpec(
        (X, Y, 1, half, strip, width),
        lambda z, place: (1, 0, lax.rem(place[1] + ZL - z, ZL), 0, 0, 0),
    )
    weight = whole((channels, channels))
    out_shape = (parts, own_rows, part_len // strip, strip, channels)
    return pl.pallas_call(
        attention_kernel,
        out_shape=jax.ShapeDtypeStruct(out_shape, jnp.bfloat16),
        grid_spec=pltpu.PrefetchScalarGridSpec(
            num_scalar_prefetch=1,
            grid=(ZL,),
            in_specs=[
                smem, whole(rows.shape), first, first, second, second,
                whole((length, 1)), whole((X, width)), whole((X, width)),
                weight, weight, weight, weight, weight,
            ],
            out_specs=whole(out_shape),
            scratch_shapes=[
                pltpu.VMEM((own_rows, channels, length), jnp.bfloat16),
                pltpu.VMEM((own_rows, length, channels), jnp.bfloat16),
            ],
        ),
        compiler_params=pltpu.CompilerParams(vmem_limit_bytes=48 << 20),
        name="attention",
    )(
        place, chain_weight, rows, near, far, near, far, chain_ids[:, None],
        chain_ids.reshape(X, width), penalty.reshape(X, width), wq, wk, wv, wg, wo,
    )


def per_device(
    pair_state,
    residue_mask,
    chain_ids,
    gain_transition,
    hidden_weight,
    out_weight,
    gain_attention,
    query_weight,
    key_weight,
    value_weight,
    gate_weight,
    bias_weight,
    chain_weight,
    output_weight,
):
    tile_rows, tile_cols, channels = pair_state.shape
    heads = chain_weight.shape[0]
    row, col = lax.axis_index("row"), lax.axis_index("col")
    my_x, my_zh = row // ZH, row % ZH
    my_zl, my_y, my_core = col // (Y * CORE), col // CORE % Y, col % CORE

    blocks = pair_state.reshape(RATIO, tile_cols, tile_cols, channels)
    got = to_mirror(jnp.stack(spread(blocks)), col, Y // 2)
    own = jnp.transpose(pair_state, (1, 0, 2))
    carried, normed, bias = transition(
        own, got, col.reshape(1), gain_transition, hidden_weight, out_weight, gain_attention,
        bias_weight,
    )

    sent = normed.reshape(ROWS, tile_cols // ROWS, tile_rows, channels)
    rows = lax.all_to_all(sent, "row", split_axis=0, concat_axis=0, tiled=True)

    by_zh = in_order(gather_shifts(bias, "row", shift_zh, ZH), my_zh)
    chunk = jnp.transpose(by_zh, (2, 1, 0, 3)).reshape(heads, tile_cols, ZH * tile_rows)
    one, two = chunk[: heads // 2], chunk[heads // 2 :]
    one = jnp.stack(gather_shifts(one, "row", shift_x, X))
    two = jnp.stack(gather_shifts(two, "col", shift_zl, ZL))
    one, two, rows = lax.optimization_barrier((one, two, rows))
    one = jnp.stack(gather_shifts(one, "col", shift_zl, ZL))
    two = jnp.stack(gather_shifts(two, "col", shift_y, Y))
    near = jnp.stack(
        gather_shifts(one, "col", shift_y, Y) + gather_shifts(two, "row", shift_x, X)
    )
    far = lax.ppermute(near, "col", shift_core(1))

    penalty = mask_penalty * (1 - residue_mask).astype(jnp.float32)
    place = jnp.stack([my_x, my_zl, my_y, my_core]).astype(jnp.int32)
    update = attention(
        rows, near, far, place, chain_weight, chain_ids, penalty,
        query_weight, key_weight, value_weight, gate_weight, output_weight,
    )
    held = lax.all_to_all(update, "row", split_axis=0, concat_axis=0, tiled=True).reshape(
        tile_cols, RATIO, tile_cols, channels
    )
    held = jnp.transpose(held, (1, 0, 2, 3))
    other = to_mirror(held, col, 0)
    back = [held[0]] + [lax.ppermute(held[m], "row", shift_x(-m)) for m in range(1, RATIO)]
    back = jnp.stack(back, axis=1).reshape(tile_cols, tile_rows, channels)
    base = jnp.transpose(2.0 * carried + back.astype(jnp.float32), (1, 0, 2))
    other = in_order(other, col % RATIO).reshape(tile_rows, tile_cols, channels)
    return (base + other.astype(jnp.float32)).astype(jnp.bfloat16)


def solution(mesh):
    placed = (P("row", "col", None),) + (P(),) * 13
    return jax.shard_map(
        per_device, mesh=mesh, in_specs=placed, out_specs=P("row", "col", None), check_vma=False
    )
```

```python
import math

import jax
import jax.numpy as jnp
from jax import lax
from jax.experimental import pallas as pl
from jax.experimental.pallas import tpu as pltpu
from jax.sharding import PartitionSpec as P

mask_penalty = 1000000000.0
norm_epsilon = 1e-05

X, ZH, ZL, Y, CORE = 4, 2, 4, 4, 2
ROWS, COLS = X * ZH, ZL * Y * CORE
RATIO = COLS // ROWS


def normalize(values, gain):
    center = values - jnp.mean(values, axis=-1, keepdims=True)
    variance = jnp.mean(center * center, axis=-1, keepdims=True)
    return center * lax.rsqrt(variance + norm_epsilon) * gain


def place_of(device):
    row, col = divmod(device, COLS)
    return row // ZH, row % ZH, col // (Y * CORE), col // CORE % Y, col % CORE


def device_of(x, zh, zl, y, core):
    return (x * ZH + zh) * COLS + (zl * Y + y) * CORE + core


def via(device, block, back=1, y_step=Y // 2):
    x, zh, zl, y, core = place_of(device)
    return device_of(
        (x + back * block) % X, zh, zl, (y + back * y_step * (block % 2)) % Y, core
    )


def out_pairs(block):
    return [(d, via(d, block)) for d in range(ROWS * COLS)]


def mirror_pairs(step, y_step):
    pairs = []
    for d in range(ROWS * COLS):
        block = (d + step) % RATIO
        row, col = divmod(via(d, block, -1, y_step), COLS)
        pairs.append((d, (col // RATIO) * COLS + RATIO * row + block))
    return pairs


def spread(blocks):
    return [blocks[0]] + [
        lax.ppermute(blocks[m], ("row", "col"), out_pairs(m)) for m in range(1, RATIO)
    ]


def to_mirror(piece, step, y_step):
    return lax.ppermute(piece, ("row", "col"), mirror_pairs(step, y_step))


def home_pairs(high, other_core):
    pairs = []
    for d in range(ROWS * COLS):
        block = CORE * high + d % CORE
        if other_core:
            block = CORE * high + 1 - d % CORE
        pairs.append((d, via(d, block, -1, 0)))
    return pairs


def shift_x(k):
    return [(r, ((r // ZH + k) % X) * ZH + r % ZH) for r in range(ROWS)]


def shift_zh(k):
    return [(r, (r // ZH) * ZH + (r + k) % ZH) for r in range(ROWS)]


def shift_zl(k):
    return [(c, (c + k * Y * CORE) % COLS) for c in range(COLS)]


def shift_y(k):
    return [
        (c, c - c % (Y * CORE) + (c + k * CORE) % (Y * CORE)) for c in range(COLS)
    ]


def shift_core(k):
    return [(c, c ^ k) for c in range(COLS)]


def gather_shifts(array, axis, pairs, count):
    return [array] + [lax.ppermute(array, axis, pairs(k)) for k in range(1, count)]


def in_order(pieces, me):
    count = len(pieces)
    twice = jnp.stack(pieces[::-1] + pieces[::-1])
    return lax.dynamic_slice_in_dim(twice, count - 1 - me, count, 0)


def transition_kernel(
    col_ref, own_ref, got0, got1, got2, got3, gain1_ref, w1_ref, w2_ref, gain2_ref, wb_ref,
    carried_ref, normed_ref, bias_ref,
):
    col = col_ref[0]
    tile_cols, tile_rows, channels = own_ref.shape
    width = tile_rows // RATIO
    for step, got in enumerate((got0, got1, got2, got3)):
        start = pl.multiple_of(lax.rem(col + RATIO - step, RATIO) * width, width)
        own = own_ref[:, pl.ds(start, width), :].astype(jnp.float32)
        sym = (own + got[...].astype(jnp.float32)).reshape(tile_cols * width, channels)
        first = normalize(sym, gain1_ref[...]).astype(jnp.bfloat16)
        hidden = jnp.maximum(
            jnp.dot(first, w1_ref[...], preferred_element_type=jnp.float32), 0.0
        ).astype(jnp.bfloat16)
        carried = sym + jnp.dot(hidden, w2_ref[...], preferred_element_type=jnp.float32)
        normed = normalize(carried, gain2_ref[...]).astype(jnp.bfloat16)
        carried_ref[:, pl.ds(start, width), :] = carried.reshape(tile_cols, width, channels)
        normed_ref[:, pl.ds(start, width), :] = normed.reshape(tile_cols, width, channels)
    for b in range(tile_cols):
        bias_ref[b] = lax.dot_general(
            wb_ref[...], normed_ref[b], (((1,), (1,)), ((), ())),
            preferred_element_type=jnp.float32,
        ).astype(jnp.bfloat16)


def transition(own, got, col, gain1, w1, w2, gain2, wb):
    tile_cols, tile_rows, channels = own.shape
    heads = wb.shape[1]
    vmem = pl.BlockSpec(memory_space=pltpu.VMEM)
    return pl.pallas_call(
        transition_kernel,
        out_shape=(
            jax.ShapeDtypeStruct(own.shape, jnp.float32),
            jax.ShapeDtypeStruct(own.shape, jnp.bfloat16),
            jax.ShapeDtypeStruct((tile_cols, heads, tile_rows), jnp.bfloat16),
        ),
        in_specs=[pl.BlockSpec(memory_space=pltpu.SMEM)] + [vmem] * 10,
        out_specs=(vmem, vmem, vmem),
        compiler_params=pltpu.CompilerParams(vmem_limit_bytes=40 << 20),
        name="transition",
    )(col, own, *got, gain1[None], w1, w2, gain2[None], wb.T)


def project_kernel(
    place_ref, rows_ref, wq_ref, wk_ref, wv_ref, wg_ref, query_ref, gate_ref, kt_ref, v_ref
):
    parts, own_rows, part_len, channels = rows_ref.shape
    my_x = place_ref[0]
    xs = [lax.rem(my_x + X - step, X) for step in range(X)]
    for i in range(own_rows):
        row = jnp.concatenate([rows_ref[x * ZH + zh, i] for x in xs for zh in range(ZH)])
        kt_ref[i] = lax.dot_general(
            wk_ref[...], row, (((0,), (1,)), ((), ())), preferred_element_type=jnp.float32
        ).astype(jnp.bfloat16)
        v_ref[i] = jnp.dot(
            row, wv_ref[...], preferred_element_type=jnp.float32
        ).astype(jnp.bfloat16)
        row = rows_ref[:, i].reshape(parts * part_len, channels)
        query = jnp.dot(row, wq_ref[...], preferred_element_type=jnp.float32)
        query_ref[:, i] = query.astype(jnp.bfloat16).reshape(parts, part_len, channels)
        gate = jax.nn.sigmoid(jnp.dot(row, wg_ref[...], preferred_element_type=jnp.float32))
        gate_ref[:, i] = gate.reshape(parts, part_len, channels)


def project(rows, place, wq, wk, wv, wg):
    parts, own_rows, part_len, channels = rows.shape
    length = parts * part_len
    vmem = pl.BlockSpec(memory_space=pltpu.VMEM)
    return pl.pallas_call(
        project_kernel,
        out_shape=(
            jax.ShapeDtypeStruct(rows.shape, jnp.bfloat16),
            jax.ShapeDtypeStruct(rows.shape, jnp.float32),
            jax.ShapeDtypeStruct((own_rows, channels, length), jnp.bfloat16),
            jax.ShapeDtypeStruct((own_rows, length, channels), jnp.bfloat16),
        ),
        in_specs=[pl.BlockSpec(memory_space=pltpu.SMEM)] + [vmem] * 5,
        out_specs=(vmem,) * 4,
        compiler_params=pltpu.CompilerParams(vmem_limit_bytes=32 << 20),
        cost_estimate=pl.CostEstimate(
            flops=8 * own_rows * length * channels * channels,
            bytes_accessed=10 * own_rows * length * channels,
            transcendentals=own_rows * length * channels,
        ),
        name="project",
    )(place, rows, wq, wk, wv, wg)


def attention_kernel(
    place_ref, cw_ref, query_ref, gate_ref, kt_ref, v_ref, a_ref, b_ref, chain_col_ref,
    chain_row_ref, penalty_ref, wo_ref, out_ref,
):
    my_x, my_zl, my_y, core = place_ref[0], place_ref[1], place_ref[2], place_ref[3]
    parts, own_rows, part_len, channels = query_ref.shape
    z_steps, half, strip = a_ref.shape[1], a_ref.shape[3], a_ref.shape[4]
    heads = 2 * half
    head_dim = channels // heads
    scale = 1.0 / math.sqrt(head_dim)
    xs = [lax.rem(my_x + X - step, X) for step in range(X)]

    per_part = part_len // strip
    places = []
    for z in range(z_steps):
        zl = lax.rem(my_zl + ZL - (pl.program_id(0) * z_steps + z), ZL)
        for y_step in range(Y):
            within = lax.rem(my_y + Y - y_step, Y) * CORE + core
            part = zl * (Y * CORE // per_part) + within // per_part
            places.append((part, lax.rem(within, per_part)))
    starts = [pl.multiple_of(block * strip, strip) for _, block in places]
    chain_rows = jnp.concatenate(
        [
            chain_col_ref[pl.ds(pl.multiple_of(part * part_len, part_len) + start, strip), :]
            for (part, _), start in zip(places, starts)
        ]
    )
    chain_keys = jnp.concatenate([chain_row_ref[pl.ds(x, 1), :] for x in xs], axis=1)
    penalty = jnp.concatenate([penalty_ref[pl.ds(x, 1), :] for x in xs], axis=1)
    same = (chain_rows == chain_keys).astype(jnp.float32)
    lane_head = lax.broadcasted_iota(jnp.int32, (1, channels), 1) // head_dim
    queries, mixes = [], []
    for i in range(own_rows):
        queries.append(
            jnp.concatenate(
                [
                    query_ref[part, i, pl.ds(start, strip), :]
                    for (part, _), start in zip(places, starts)
                ]
            )
        )
        mixes.append(jnp.zeros((len(places) * strip, channels), jnp.float32))
    for h in range(heads):
        strips = []
        for z in range(z_steps):
            for y_step in range(Y):
                if h < half:
                    chunks = [a_ref[y_step, z, k, h] for k in range(X)]
                else:
                    chunks = [b_ref[k, y_step, z, h - half] for k in range(X)]
                strips.append(jnp.concatenate(chunks, axis=1))
        pair = jnp.concatenate(strips).astype(jnp.float32)
        full = pair + cw_ref[h] * same - penalty
        mine = lane_head == h
        for i in range(own_rows):
            query = jnp.where(mine, queries[i], jnp.zeros_like(queries[i]))
            scores = (
                jnp.dot(query, kt_ref[i], preferred_element_type=jnp.float32) * scale + full
            )
            exponent = jnp.exp(scores - jnp.max(scores, axis=-1, keepdims=True))
            weights = (
                exponent * (1.0 / jnp.sum(exponent, axis=-1, keepdims=True))
            ).astype(jnp.bfloat16)
            mix = jnp.dot(weights, v_ref[i], preferred_element_type=jnp.float32)
            mixes[i] = jnp.where(mine, mix, mixes[i])
    for i in range(own_rows):
        gate = jnp.concatenate(
            [
                gate_ref[part, i, pl.ds(start, strip), :]
                for (part, _), start in zip(places, starts)
            ]
        )
        gated = (gate * mixes[i]).astype(jnp.bfloat16)
        update = jnp.dot(gated, wo_ref[...], preferred_element_type=jnp.float32).astype(
            jnp.bfloat16
        )
        for n, (part, block) in enumerate(places):
            to = lax.rem(part // ZH + block, X) * ZH + lax.rem(part, ZH)
            out_ref[to, i, block // CORE] = update[n * strip : (n + 1) * strip]


def attention(projected, bias, place, chain_weight, chain_ids, penalty, wo):
    parts, own_rows, part_len, channels = projected[0].shape
    half, strip, width = bias.shape[3:]
    length = parts * part_len
    z_steps = ZL // 2
    smem = pl.BlockSpec(memory_space=pltpu.SMEM)

    def whole(shape):
        return pl.BlockSpec(shape, lambda g: (0,) * len(shape))

    first = pl.BlockSpec((Y, z_steps, X, half, strip, width), lambda g: (0, g, 0, 0, 0, 0))
    second = pl.BlockSpec((X, Y, z_steps, half, strip, width), lambda g: (1, 0, g, 0, 0, 0))
    out_shape = (parts, own_rows, part_len // strip // CORE, strip, channels)
    scores = own_rows * length // CORE * length * 2 * half
    return pl.pallas_call(
        attention_kernel,
        out_shape=jax.ShapeDtypeStruct(out_shape, jnp.bfloat16),
        grid=(ZL // z_steps,),
        in_specs=[smem, smem]
        + [whole(p.shape) for p in projected]
        + [
            first, second, whole((length, 1)), whole((X, width)), whole((X, width)),
            whole(wo.shape),
        ],
        out_specs=whole(out_shape),
        compiler_params=pltpu.CompilerParams(vmem_limit_bytes=48 << 20),
        cost_estimate=pl.CostEstimate(
            flops=4 * scores * channels,
            bytes_accessed=2 * scores // own_rows + 10 * own_rows * length * channels,
            transcendentals=scores,
        ),
        name="attention",
    )(
        place, chain_weight, *projected, bias, bias, chain_ids[:, None],
        chain_ids.reshape(X, width), penalty.reshape(X, width), wo,
    )


def per_device(
    pair_state,
    residue_mask,
    chain_ids,
    gain_transition,
    hidden_weight,
    out_weight,
    gain_attention,
    query_weight,
    key_weight,
    value_weight,
    gate_weight,
    bias_weight,
    chain_weight,
    output_weight,
):
    tile_rows, tile_cols, channels = pair_state.shape
    heads = chain_weight.shape[0]
    row, col = lax.axis_index("row"), lax.axis_index("col")
    my_x, my_zh = row // ZH, row % ZH
    my_zl, my_y, my_core = col // (Y * CORE), col // CORE % Y, col % CORE

    blocks = pair_state.reshape(RATIO, tile_cols, tile_cols, channels)
    held = jnp.stack(spread(blocks))
    got = [
        to_mirror(
            lax.dynamic_index_in_dim(held, (col + step) % RATIO, 0, keepdims=False), step, Y // 2
        )
        for step in range(RATIO)
    ]
    own = jnp.transpose(pair_state, (1, 0, 2))
    carried, normed, bias = transition(
        own, got, col.reshape(1), gain_transition, hidden_weight, out_weight, gain_attention,
        bias_weight,
    )

    sent = normed.reshape(ROWS, tile_cols // ROWS, tile_rows, channels)
    rows = lax.all_to_all(sent, "row", split_axis=0, concat_axis=0, tiled=True)

    by_zh = in_order(gather_shifts(bias, "row", shift_zh, ZH), my_zh)
    chunk = jnp.transpose(by_zh, (2, 1, 0, 3)).reshape(heads, tile_cols, ZH * tile_rows)
    one, two = chunk[: heads // 2], chunk[heads // 2 :]
    one = jnp.stack(gather_shifts(one, "row", shift_x, X))
    two = jnp.stack(gather_shifts(two, "col", shift_zl, ZL))
    one, two, rows = lax.optimization_barrier((one, two, rows))
    one = jnp.stack(gather_shifts(one, "col", shift_zl, ZL))
    two = jnp.stack(gather_shifts(two, "col", shift_y, Y))
    penalty = mask_penalty * (1 - residue_mask).astype(jnp.float32)
    place = jnp.stack([my_x, my_zl, my_y, my_core]).astype(jnp.int32)
    other_place = jnp.stack([my_x, my_zl, my_y, 1 - my_core]).astype(jnp.int32)
    projected = project(rows, place, query_weight, key_weight, value_weight, gate_weight)
    one, two, projected = lax.optimization_barrier((one, two, projected))
    near = jnp.stack(
        gather_shifts(one, "col", shift_y, Y) + gather_shifts(two, "row", shift_x, X)
    )
    far = lax.ppermute(near, "col", shift_core(1))

    other, home = {}, []
    for turn, where in enumerate((place, other_place)):
        update = attention(
            projected, far if turn else near, where, chain_weight, chain_ids, penalty, output_weight
        )
        if turn == 0:
            far, _ = lax.optimization_barrier((far, update))
        else:
            update, _ = lax.optimization_barrier((update, held))
        held = lax.all_to_all(update, "row", split_axis=0, concat_axis=0, tiled=True).reshape(
            tile_cols, RATIO // CORE, tile_cols, channels
        )
        for step in range(turn, RATIO, CORE):
            piece = lax.dynamic_index_in_dim(
                held, (col + step) % RATIO // CORE, 1, keepdims=False
            )
            other[step] = to_mirror(piece, step, 0)
        home.append(
            [
                lax.ppermute(held[:, high], ("row", "col"), home_pairs(high, turn == 1))
                for high in range(RATIO // CORE)
            ]
        )
    back = []
    for high in range(RATIO // CORE):
        mine, others = home[0][high], home[1][high]
        back.append(jnp.where(my_core == 0, mine, others))
        back.append(jnp.where(my_core == 0, others, mine))
    back = jnp.stack(back, axis=1).reshape(tile_cols, tile_rows, channels)
    base = jnp.transpose(2.0 * carried + back.astype(jnp.float32), (1, 0, 2))
    other = in_order([other[step] for step in range(RATIO)], col % RATIO)
    other = other.reshape(tile_rows, tile_cols, channels)
    return (base + other.astype(jnp.float32)).astype(jnp.bfloat16)


def solution(mesh):
    placed = (P("row", "col", None),) + (P(),) * 13
    return jax.shard_map(
        per_device, mesh=mesh, in_specs=placed, out_specs=P("row", "col", None), check_vma=False
    )
```

```python
import math

import jax
import jax.numpy as jnp
from jax import lax
from jax.experimental import pallas as pl
from jax.experimental.pallas import tpu as pltpu
from jax.sharding import PartitionSpec as P

mask_penalty = 1000000000.0
norm_epsilon = 1e-05

X, ZH, ZL, Y, CORE = 4, 2, 4, 4, 2
ROWS, COLS = X * ZH, ZL * Y * CORE
RATIO = COLS // ROWS


def normalize(values, gain):
    center = values - jnp.mean(values, axis=-1, keepdims=True)
    variance = jnp.mean(center * center, axis=-1, keepdims=True)
    return center * lax.rsqrt(variance + norm_epsilon) * gain


def place_of(device):
    row, col = divmod(device, COLS)
    return row // ZH, row % ZH, col // (Y * CORE), col // CORE % Y, col % CORE


def device_of(x, zh, zl, y, core):
    return (x * ZH + zh) * COLS + (zl * Y + y) * CORE + core


def via(device, block, back=1, y_step=Y // 2):
    x, zh, zl, y, core = place_of(device)
    return device_of(
        (x + back * block) % X, zh, zl, (y + back * y_step * (block % 2)) % Y, core
    )


def out_pairs(block):
    return [(d, via(d, block)) for d in range(ROWS * COLS)]


def mirror_pairs(step, y_step):
    pairs = []
    for d in range(ROWS * COLS):
        block = (d + step) % RATIO
        row, col = divmod(via(d, block, -1, y_step), COLS)
        pairs.append((d, (col // RATIO) * COLS + RATIO * row + block))
    return pairs


def spread(blocks):
    return [blocks[0]] + [
        lax.ppermute(blocks[m], ("row", "col"), out_pairs(m)) for m in range(1, RATIO)
    ]


def to_mirror(piece, step, y_step):
    return lax.ppermute(piece, ("row", "col"), mirror_pairs(step, y_step))


def shift_x(k):
    return [(r, ((r // ZH + k) % X) * ZH + r % ZH) for r in range(ROWS)]


def shift_zh(k):
    return [(r, (r // ZH) * ZH + (r + k) % ZH) for r in range(ROWS)]


def shift_zl(k):
    return [(c, (c + k * Y * CORE) % COLS) for c in range(COLS)]


def shift_y(k):
    return [
        (c, c - c % (Y * CORE) + (c + k * CORE) % (Y * CORE)) for c in range(COLS)
    ]


def shift_core(k):
    return [(c, c ^ k) for c in range(COLS)]


def gather_shifts(array, axis, pairs, count):
    return [array] + [lax.ppermute(array, axis, pairs(k)) for k in range(1, count)]


def in_order(pieces, me):
    count = len(pieces)
    twice = jnp.stack(pieces[::-1] + pieces[::-1])
    return lax.dynamic_slice_in_dim(twice, count - 1 - me, count, 0)


def transition_kernel(
    col_ref, own_ref, got0, got1, got2, got3, gain1_ref, w1_ref, w2_ref, gain2_ref, wb_ref,
    carried_ref, normed_ref, bias_ref,
):
    col = col_ref[0]
    tile_cols, tile_rows, channels = own_ref.shape
    width = tile_rows // RATIO
    for step, got in enumerate((got0, got1, got2, got3)):
        start = pl.multiple_of(lax.rem(col + RATIO - step, RATIO) * width, width)
        own = own_ref[:, pl.ds(start, width), :].astype(jnp.float32)
        sym = (own + got[...].astype(jnp.float32)).reshape(tile_cols * width, channels)
        first = normalize(sym, gain1_ref[...]).astype(jnp.bfloat16)
        hidden = jnp.maximum(
            jnp.dot(first, w1_ref[...], preferred_element_type=jnp.float32), 0.0
        ).astype(jnp.bfloat16)
        carried = sym + jnp.dot(hidden, w2_ref[...], preferred_element_type=jnp.float32)
        normed = normalize(carried, gain2_ref[...]).astype(jnp.bfloat16)
        carried_ref[:, pl.ds(start, width), :] = carried.reshape(tile_cols, width, channels)
        normed_ref[:, pl.ds(start, width), :] = normed.reshape(tile_cols, width, channels)
    for b in range(tile_cols):
        bias_ref[b] = lax.dot_general(
            wb_ref[...], normed_ref[b], (((1,), (1,)), ((), ())),
            preferred_element_type=jnp.float32,
        ).astype(jnp.bfloat16)


def transition(own, got, col, gain1, w1, w2, gain2, wb):
    tile_cols, tile_rows, channels = own.shape
    heads = wb.shape[1]
    vmem = pl.BlockSpec(memory_space=pltpu.VMEM)
    return pl.pallas_call(
        transition_kernel,
        out_shape=(
            jax.ShapeDtypeStruct(own.shape, jnp.float32),
            jax.ShapeDtypeStruct(own.shape, jnp.bfloat16),
            jax.ShapeDtypeStruct((tile_cols, heads, tile_rows), jnp.bfloat16),
        ),
        in_specs=[pl.BlockSpec(memory_space=pltpu.SMEM)] + [vmem] * 10,
        out_specs=(vmem, vmem, vmem),
        compiler_params=pltpu.CompilerParams(vmem_limit_bytes=24 << 20),
        name="transition",
    )(col, own, *got, gain1[None], w1, w2, gain2[None], wb.T)


def attention_kernel(
    place_ref, cw_ref, rows_ref, wq_ref, wk_ref, wv_ref, wg_ref, wo_ref, a_ref, b_ref,
    chain_col_ref, chain_row_ref, penalty_ref, *refs,
):
    begun_refs, (out_ref, kt_ref, v_ref) = refs[:-3], refs[-3:]
    my_x, my_zl, my_y, core = place_ref[0], place_ref[1], place_ref[2], place_ref[3]
    parts, own_rows, part_len, channels = rows_ref.shape
    z_steps, half, strip = a_ref.shape[1], a_ref.shape[3], a_ref.shape[4]
    heads = 2 * half
    head_dim = channels // heads
    scale = 1.0 / math.sqrt(head_dim)
    xs = [lax.rem(my_x + X - step, X) for step in range(X)]

    @pl.when(pl.program_id(0) == 0)
    def _():
        for begun_ref in begun_refs:
            out_ref[...] = begun_ref[...]
        for i in range(own_rows):
            row = jnp.concatenate([rows_ref[x * ZH + zh, i] for x in xs for zh in range(ZH)])
            kt_ref[i] = lax.dot_general(
                wk_ref[...], row, (((0,), (1,)), ((), ())), preferred_element_type=jnp.float32
            ).astype(jnp.bfloat16)
            v_ref[i] = jnp.dot(
                row, wv_ref[...], preferred_element_type=jnp.float32
            ).astype(jnp.bfloat16)

    per_part = part_len // strip
    places = []
    for z in range(z_steps):
        zl = lax.rem(my_zl + ZL - (pl.program_id(0) * z_steps + z), ZL)
        for y_step in range(Y):
            within = lax.rem(my_y + Y - y_step, Y) * CORE + core
            part = zl * (Y * CORE // per_part) + within // per_part
            places.append((part, lax.rem(within, per_part)))
    starts = [pl.multiple_of(block * strip, strip) for _, block in places]
    chain_rows = jnp.concatenate(
        [
            chain_col_ref[pl.ds(pl.multiple_of(part * part_len, part_len) + start, strip), :]
            for (part, _), start in zip(places, starts)
        ]
    )
    chain_keys = jnp.concatenate([chain_row_ref[pl.ds(x, 1), :] for x in xs], axis=1)
    penalty = jnp.concatenate([penalty_ref[pl.ds(x, 1), :] for x in xs], axis=1)
    same = (chain_rows == chain_keys).astype(jnp.float32)
    lane_head = lax.broadcasted_iota(jnp.int32, (1, channels), 1) // head_dim
    queries, gates, mixes = [], [], []
    for i in range(own_rows):
        part_rows = jnp.concatenate(
            [rows_ref[part, i, pl.ds(start, strip), :] for (part, _), start in zip(places, starts)]
        )
        queries.append(
            jnp.dot(part_rows, wq_ref[...], preferred_element_type=jnp.float32).astype(jnp.bfloat16)
        )
        gates.append(
            jax.nn.sigmoid(jnp.dot(part_rows, wg_ref[...], preferred_element_type=jnp.float32))
        )
        mixes.append(jnp.zeros((len(places) * strip, channels), jnp.float32))
    for h in range(heads):
        strips = []
        for z in range(z_steps):
            for y_step in range(Y):
                if h < half:
                    chunks = [a_ref[y_step, z, k, h] for k in range(X)]
                else:
                    chunks = [b_ref[k, y_step, z, h - half] for k in range(X)]
                strips.append(jnp.concatenate(chunks, axis=1))
        pair = jnp.concatenate(strips).astype(jnp.float32)
        full = pair + cw_ref[h] * same - penalty
        mine = lane_head == h
        for i in range(own_rows):
            query = jnp.where(mine, queries[i], jnp.zeros_like(queries[i]))
            scores = (
                jnp.dot(query, kt_ref[i], preferred_element_type=jnp.float32) * scale + full
            )
            exponent = jnp.exp(scores - jnp.max(scores, axis=-1, keepdims=True))
            weights = (
                exponent * (1.0 / jnp.sum(exponent, axis=-1, keepdims=True))
            ).astype(jnp.bfloat16)
            mix = jnp.dot(weights, v_ref[i], preferred_element_type=jnp.float32)
            mixes[i] = jnp.where(mine, mix, mixes[i])
    for i in range(own_rows):
        gated = (gates[i] * mixes[i]).astype(jnp.bfloat16)
        update = jnp.dot(gated, wo_ref[...], preferred_element_type=jnp.float32).astype(
            jnp.bfloat16
        )
        for n, (part, block) in enumerate(places):
            to = lax.rem(part // ZH + block, X) * ZH + lax.rem(part, ZH)
            out_ref[to, i, block] = update[n * strip : (n + 1) * strip]


def attention(rows, weights, bias, place, chain_weight, chain_ids, penalty, begun=None):
    parts, own_rows, part_len, channels = rows.shape
    half, strip, width = bias.shape[3:]
    length = parts * part_len
    z_steps = ZL // 2
    smem = pl.BlockSpec(memory_space=pltpu.SMEM)

    def whole(shape):
        return pl.BlockSpec(shape, lambda g: (0,) * len(shape))

    first = pl.BlockSpec((Y, z_steps, X, half, strip, width), lambda g: (0, g, 0, 0, 0, 0))
    second = pl.BlockSpec((X, Y, z_steps, half, strip, width), lambda g: (1, 0, g, 0, 0, 0))
    out_shape = (parts, own_rows, part_len // strip, strip, channels)
    begun = [] if begun is None else [begun]
    scores = own_rows * length // CORE * length * 2 * half
    return pl.pallas_call(
        attention_kernel,
        out_shape=jax.ShapeDtypeStruct(out_shape, jnp.bfloat16),
        grid=(ZL // z_steps,),
        in_specs=[smem, smem, whole(rows.shape)]
        + [whole(w.shape) for w in weights]
        + [first, second, whole((length, 1)), whole((X, width)), whole((X, width))]
        + [whole(out_shape)] * len(begun),
        out_specs=whole(out_shape),
        scratch_shapes=[
            pltpu.VMEM((own_rows, channels, length), jnp.bfloat16),
            pltpu.VMEM((own_rows, length, channels), jnp.bfloat16),
        ],
        compiler_params=pltpu.CompilerParams(vmem_limit_bytes=20 << 20),
        cost_estimate=pl.CostEstimate(
            flops=4 * scores * channels,
            bytes_accessed=2 * scores // own_rows + 10 * own_rows * length * channels,
            transcendentals=scores,
        ),
        name="attention",
    )(
        place, chain_weight, rows, *weights, bias, bias, chain_ids[:, None],
        chain_ids.reshape(X, width), penalty.reshape(X, width), *begun,
    )


def per_device(
    pair_state,
    residue_mask,
    chain_ids,
    gain_transition,
    hidden_weight,
    out_weight,
    gain_attention,
    query_weight,
    key_weight,
    value_weight,
    gate_weight,
    bias_weight,
    chain_weight,
    output_weight,
):
    tile_rows, tile_cols, channels = pair_state.shape
    heads = chain_weight.shape[0]
    row, col = lax.axis_index("row"), lax.axis_index("col")
    my_x, my_zh = row // ZH, row % ZH
    my_zl, my_y, my_core = col // (Y * CORE), col // CORE % Y, col % CORE

    blocks = pair_state.reshape(RATIO, tile_cols, tile_cols, channels)
    held = jnp.stack(spread(blocks))
    got = [
        to_mirror(
            lax.dynamic_index_in_dim(held, (col + step) % RATIO, 0, keepdims=False), step, Y // 2
        )
        for step in range(RATIO)
    ]
    own = jnp.transpose(pair_state, (1, 0, 2))
    carried, normed, bias = transition(
        own, got, col.reshape(1), gain_transition, hidden_weight, out_weight, gain_attention,
        bias_weight,
    )

    by_zh = in_order(gather_shifts(bias, "row", shift_zh, ZH), my_zh)
    chunk = jnp.transpose(by_zh, (2, 1, 0, 3)).reshape(heads, tile_cols, ZH * tile_rows)
    one, two = chunk[: heads // 2], chunk[heads // 2 :]
    one = jnp.stack(gather_shifts(one, "row", shift_x, X))
    two = jnp.stack(gather_shifts(two, "col", shift_zl, ZL))

    sent = normed.reshape(ROWS, tile_cols // ROWS, tile_rows, channels)
    sent, _ = lax.optimization_barrier((sent, by_zh))
    rows = lax.all_to_all(sent, "row", split_axis=0, concat_axis=0, tiled=True)

    one = jnp.stack(gather_shifts(one, "col", shift_zl, ZL))
    two = jnp.stack(gather_shifts(two, "col", shift_y, Y))
    penalty = mask_penalty * (1 - residue_mask).astype(jnp.float32)
    place = jnp.stack([my_x, my_zl, my_y, my_core]).astype(jnp.int32)
    other_place = jnp.stack([my_x, my_zl, my_y, 1 - my_core]).astype(jnp.int32)
    one, two, rows, place, other_place, penalty = lax.optimization_barrier(
        (one, two, rows, place, other_place, penalty)
    )
    near = jnp.stack(
        gather_shifts(one, "col", shift_y, Y) + gather_shifts(two, "row", shift_x, X)
    )
    far = lax.ppermute(near, "col", shift_core(1))

    weights = (query_weight, key_weight, value_weight, gate_weight, output_weight)
    mine = attention(rows, weights, near, place, chain_weight, chain_ids, penalty)
    far, _ = lax.optimization_barrier((far, mine))
    update = attention(rows, weights, far, other_place, chain_weight, chain_ids, penalty, mine)
    held = lax.all_to_all(update, "row", split_axis=0, concat_axis=0, tiled=True).reshape(
        tile_cols, RATIO, tile_cols, channels
    )
    held = jnp.transpose(held, (1, 0, 2, 3))
    other = [
        to_mirror(lax.dynamic_index_in_dim(held, (col + step) % RATIO, 0, keepdims=False), step, 0)
        for step in range(RATIO)
    ]
    back = [held[0]] + [lax.ppermute(held[m], "row", shift_x(-m)) for m in range(1, RATIO)]
    back = jnp.stack(back, axis=1).reshape(tile_cols, tile_rows, channels)
    base = jnp.transpose(2.0 * carried + back.astype(jnp.float32), (1, 0, 2))
    other = in_order(other, col % RATIO).reshape(tile_rows, tile_cols, channels)
    return (base + other.astype(jnp.float32)).astype(jnp.bfloat16)


def solution(mesh):
    placed = (P("row", "col", None),) + (P(),) * 13
    return jax.shard_map(
        per_device, mesh=mesh, in_specs=placed, out_specs=P("row", "col", None), check_vma=False
    )
```

```python
import math

import jax
import jax.numpy as jnp
from jax import lax
from jax.experimental import pallas as pl
from jax.experimental.pallas import tpu as pltpu
from jax.sharding import PartitionSpec as P

mask_penalty = 1000000000.0
norm_epsilon = 1e-05

X, ZH, ZL, Y, CORE = 4, 2, 4, 4, 2
ROWS, COLS = X * ZH, ZL * Y * CORE
RATIO = COLS // ROWS


def normalize(values, gain):
    center = values - jnp.mean(values, axis=-1, keepdims=True)
    variance = jnp.mean(center * center, axis=-1, keepdims=True)
    return center * lax.rsqrt(variance + norm_epsilon) * gain


def place_of(device):
    row, col = divmod(device, COLS)
    return row // ZH, row % ZH, col // (Y * CORE), col // CORE % Y, col % CORE


def device_of(x, zh, zl, y, core):
    return (x * ZH + zh) * COLS + (zl * Y + y) * CORE + core


def via(device, block, back=1, y_step=Y // 2):
    x, zh, zl, y, core = place_of(device)
    return device_of(
        (x + back * block) % X, zh, zl, (y + back * y_step * (block % 2)) % Y, core
    )


def out_pairs(block):
    return [(d, via(d, block)) for d in range(ROWS * COLS)]


def mirror_pairs(step, y_step):
    pairs = []
    for d in range(ROWS * COLS):
        block = (d + step) % RATIO
        row, col = divmod(via(d, block, -1, y_step), COLS)
        pairs.append((d, (col // RATIO) * COLS + RATIO * row + block))
    return pairs


def spread(blocks):
    return [blocks[0]] + [
        lax.ppermute(blocks[m], ("row", "col"), out_pairs(m)) for m in range(1, RATIO)
    ]


def to_mirror(piece, step, y_step):
    return lax.ppermute(piece, ("row", "col"), mirror_pairs(step, y_step))


def shift_x(k):
    return [(r, ((r // ZH + k) % X) * ZH + r % ZH) for r in range(ROWS)]


def shift_zh(k):
    return [(r, (r // ZH) * ZH + (r + k) % ZH) for r in range(ROWS)]


def shift_zl(k):
    return [(c, (c + k * Y * CORE) % COLS) for c in range(COLS)]


def shift_y(k):
    return [
        (c, c - c % (Y * CORE) + (c + k * CORE) % (Y * CORE)) for c in range(COLS)
    ]


def shift_core(k):
    return [(c, c ^ k) for c in range(COLS)]


def gather_shifts(array, axis, pairs, count):
    return [array] + [lax.ppermute(array, axis, pairs(k)) for k in range(1, count)]


def in_order(pieces, me):
    count = len(pieces)
    twice = jnp.stack(pieces[::-1] + pieces[::-1])
    return lax.dynamic_slice_in_dim(twice, count - 1 - me, count, 0)


def transition_kernel(
    col_ref, own_ref, got0, got1, got2, got3, gain1_ref, w1_ref, w2_ref, gain2_ref, wb_ref,
    carried_ref, normed_ref, bias_ref,
):
    col = col_ref[0]
    tile_cols, tile_rows, channels = own_ref.shape
    width = tile_rows // RATIO
    for step, got in enumerate((got0, got1, got2, got3)):
        start = pl.multiple_of(lax.rem(col + RATIO - step, RATIO) * width, width)
        own = own_ref[:, pl.ds(start, width), :].astype(jnp.float32)
        sym = (own + got[...].astype(jnp.float32)).reshape(tile_cols * width, channels)
        first = normalize(sym, gain1_ref[...]).astype(jnp.bfloat16)
        hidden = jnp.maximum(
            jnp.dot(first, w1_ref[...], preferred_element_type=jnp.float32), 0.0
        ).astype(jnp.bfloat16)
        carried = sym + jnp.dot(hidden, w2_ref[...], preferred_element_type=jnp.float32)
        normed = normalize(carried, gain2_ref[...]).astype(jnp.bfloat16)
        carried_ref[:, pl.ds(start, width), :] = carried.reshape(tile_cols, width, channels)
        normed_ref[:, pl.ds(start, width), :] = normed.reshape(tile_cols, width, channels)
    for b in range(tile_cols):
        bias_ref[b] = lax.dot_general(
            wb_ref[...], normed_ref[b], (((1,), (1,)), ((), ())),
            preferred_element_type=jnp.float32,
        ).astype(jnp.bfloat16)


def transition(own, got, col, gain1, w1, w2, gain2, wb):
    tile_cols, tile_rows, channels = own.shape
    heads = wb.shape[1]
    vmem = pl.BlockSpec(memory_space=pltpu.VMEM)
    return pl.pallas_call(
        transition_kernel,
        out_shape=(
            jax.ShapeDtypeStruct(own.shape, jnp.float32),
            jax.ShapeDtypeStruct(own.shape, jnp.bfloat16),
            jax.ShapeDtypeStruct((tile_cols, heads, tile_rows), jnp.bfloat16),
        ),
        in_specs=[pl.BlockSpec(memory_space=pltpu.SMEM)] + [vmem] * 10,
        out_specs=(vmem, vmem, vmem),
        compiler_params=pltpu.CompilerParams(vmem_limit_bytes=24 << 20),
        name="transition",
    )(col, own, *got, gain1[None], w1, w2, gain2[None], wb.T)


def attention_kernel(
    place_ref, cw_ref, rows_ref, wq_ref, wk_ref, wv_ref, wg_ref, wo_ref, a_ref, b_ref,
    chain_col_ref, chain_row_ref, penalty_ref, *refs,
):
    begun_refs, (out_ref, kt_ref, v_ref) = refs[:-3], refs[-3:]
    my_x, my_zl, my_y, core = place_ref[0], place_ref[1], place_ref[2], place_ref[3]
    parts, own_rows, part_len, channels = rows_ref.shape
    z_steps, half, strip = a_ref.shape[1], a_ref.shape[3], a_ref.shape[4]
    heads = 2 * half
    head_dim = channels // heads
    scale = 1.0 / math.sqrt(head_dim)
    xs = [lax.rem(my_x + X - step, X) for step in range(X)]

    @pl.when(pl.program_id(0) == 0)
    def _():
        for begun_ref in begun_refs:
            out_ref[...] = begun_ref[...]
        for i in range(own_rows):
            row = jnp.concatenate([rows_ref[x * ZH + zh, i] for x in xs for zh in range(ZH)])
            kt_ref[i] = lax.dot_general(
                wk_ref[...], row, (((0,), (1,)), ((), ())), preferred_element_type=jnp.float32
            ).astype(jnp.bfloat16)
            v_ref[i] = jnp.dot(
                row, wv_ref[...], preferred_element_type=jnp.float32
            ).astype(jnp.bfloat16)

    per_part = part_len // strip
    places = []
    for z in range(z_steps):
        zl = lax.rem(my_zl + ZL - (pl.program_id(0) * z_steps + z), ZL)
        for y_step in range(Y):
            within = lax.rem(my_y + Y - y_step, Y) * CORE + core
            part = zl * (Y * CORE // per_part) + within // per_part
            places.append((part, lax.rem(within, per_part)))
    starts = [pl.multiple_of(block * strip, strip) for _, block in places]
    chain_rows = jnp.concatenate(
        [
            chain_col_ref[pl.ds(pl.multiple_of(part * part_len, part_len) + start, strip), :]
            for (part, _), start in zip(places, starts)
        ]
    )
    chain_keys = jnp.concatenate([chain_row_ref[pl.ds(x, 1), :] for x in xs], axis=1)
    penalty = jnp.concatenate([penalty_ref[pl.ds(x, 1), :] for x in xs], axis=1)
    same = (chain_rows == chain_keys).astype(jnp.float32)
    lane_head = lax.broadcasted_iota(jnp.int32, (1, channels), 1) // head_dim
    queries, gates, mixes = [], [], []
    for i in range(own_rows):
        part_rows = jnp.concatenate(
            [rows_ref[part, i, pl.ds(start, strip), :] for (part, _), start in zip(places, starts)]
        )
        queries.append(
            jnp.dot(part_rows, wq_ref[...], preferred_element_type=jnp.float32).astype(jnp.bfloat16)
        )
        gates.append(
            jax.nn.sigmoid(jnp.dot(part_rows, wg_ref[...], preferred_element_type=jnp.float32))
        )
        mixes.append(jnp.zeros((len(places) * strip, channels), jnp.float32))
    count = len(places) * strip
    masked = [lane_head == h for h in range(heads)]
    products = [
        jnp.dot(
            jnp.concatenate(
                [jnp.where(mine, query, jnp.zeros_like(query)) for mine in masked]
            ),
            kt_ref[i],
            preferred_element_type=jnp.float32,
        )
        for i, query in enumerate(queries)
    ]
    weights = [[] for _ in range(own_rows)]
    for h in range(heads):
        strips = []
        for z in range(z_steps):
            for y_step in range(Y):
                if h < half:
                    chunks = [a_ref[y_step, z, k, h] for k in range(X)]
                else:
                    chunks = [b_ref[k, y_step, z, h - half] for k in range(X)]
                strips.append(jnp.concatenate(chunks, axis=1))
        pair = jnp.concatenate(strips).astype(jnp.float32)
        full = pair + cw_ref[h] * same - penalty
        for i in range(own_rows):
            scores = products[i][h * count : (h + 1) * count] * scale + full
            exponent = jnp.exp(scores - jnp.max(scores, axis=-1, keepdims=True))
            weights[i].append(
                (exponent * (1.0 / jnp.sum(exponent, axis=-1, keepdims=True))).astype(
                    jnp.bfloat16
                )
            )
    for i in range(own_rows):
        mixed = jnp.dot(
            jnp.concatenate(weights[i]), v_ref[i], preferred_element_type=jnp.float32
        )
        for h, mine in enumerate(masked):
            mixes[i] = jnp.where(mine, mixed[h * count : (h + 1) * count], mixes[i])
    for i in range(own_rows):
        gated = (gates[i] * mixes[i]).astype(jnp.bfloat16)
        update = jnp.dot(gated, wo_ref[...], preferred_element_type=jnp.float32).astype(
            jnp.bfloat16
        )
        for n, (part, block) in enumerate(places):
            to = lax.rem(part // ZH + block, X) * ZH + lax.rem(part, ZH)
            out_ref[to, i, block] = update[n * strip : (n + 1) * strip]


def attention(rows, weights, bias, place, chain_weight, chain_ids, penalty, begun=None):
    parts, own_rows, part_len, channels = rows.shape
    half, strip, width = bias.shape[3:]
    length = parts * part_len
    z_steps = ZL
    smem = pl.BlockSpec(memory_space=pltpu.SMEM)

    def whole(shape):
        return pl.BlockSpec(shape, lambda g: (0,) * len(shape))

    first = pl.BlockSpec((Y, z_steps, X, half, strip, width), lambda g: (0, g, 0, 0, 0, 0))
    second = pl.BlockSpec((X, Y, z_steps, half, strip, width), lambda g: (1, 0, g, 0, 0, 0))
    out_shape = (parts, own_rows, part_len // strip, strip, channels)
    begun = [] if begun is None else [begun]
    scores = own_rows * length // CORE * length * 2 * half
    return pl.pallas_call(
        attention_kernel,
        out_shape=jax.ShapeDtypeStruct(out_shape, jnp.bfloat16),
        grid=(ZL // z_steps,),
        in_specs=[smem, smem, whole(rows.shape)]
        + [whole(w.shape) for w in weights]
        + [first, second, whole((length, 1)), whole((X, width)), whole((X, width))]
        + [whole(out_shape)] * len(begun),
        out_specs=whole(out_shape),
        scratch_shapes=[
            pltpu.VMEM((own_rows, channels, length), jnp.bfloat16),
            pltpu.VMEM((own_rows, length, channels), jnp.bfloat16),
        ],
        compiler_params=pltpu.CompilerParams(vmem_limit_bytes=28 << 20),
        cost_estimate=pl.CostEstimate(
            flops=4 * scores * channels,
            bytes_accessed=2 * scores // own_rows + 10 * own_rows * length * channels,
            transcendentals=scores,
        ),
        name="attention",
    )(
        place, chain_weight, rows, *weights, bias, bias, chain_ids[:, None],
        chain_ids.reshape(X, width), penalty.reshape(X, width), *begun,
    )


def per_device(
    pair_state,
    residue_mask,
    chain_ids,
    gain_transition,
    hidden_weight,
    out_weight,
    gain_attention,
    query_weight,
    key_weight,
    value_weight,
    gate_weight,
    bias_weight,
    chain_weight,
    output_weight,
):
    tile_rows, tile_cols, channels = pair_state.shape
    heads = chain_weight.shape[0]
    row, col = lax.axis_index("row"), lax.axis_index("col")
    my_x, my_zh = row // ZH, row % ZH
    my_zl, my_y, my_core = col // (Y * CORE), col // CORE % Y, col % CORE

    blocks = pair_state.reshape(RATIO, tile_cols, tile_cols, channels)
    held = jnp.stack(spread(blocks))
    got = [
        to_mirror(
            lax.dynamic_index_in_dim(held, (col + step) % RATIO, 0, keepdims=False), step, Y // 2
        )
        for step in range(RATIO)
    ]
    own = jnp.transpose(pair_state, (1, 0, 2))
    carried, normed, bias = transition(
        own, got, col.reshape(1), gain_transition, hidden_weight, out_weight, gain_attention,
        bias_weight,
    )

    by_zh = in_order(gather_shifts(bias, "row", shift_zh, ZH), my_zh)
    chunk = jnp.transpose(by_zh, (2, 1, 0, 3)).reshape(heads, tile_cols, ZH * tile_rows)
    one, two = chunk[: heads // 2], chunk[heads // 2 :]
    by_x = gather_shifts(one, "row", shift_x, X)
    by_zl = gather_shifts(two, "col", shift_zl, ZL)
    one, two = jnp.stack(by_x), jnp.stack(by_zl)

    sent = normed.reshape(ROWS, tile_cols // ROWS, tile_rows, channels)
    sent, _, _ = lax.optimization_barrier((sent, one, two))
    rows = lax.all_to_all(sent, "row", split_axis=0, concat_axis=0, tiled=True)

    one = jnp.stack(gather_shifts(one, "col", shift_zl, ZL))
    two = jnp.stack(gather_shifts(two, "col", shift_y, Y))
    penalty = mask_penalty * (1 - residue_mask).astype(jnp.float32)
    place = jnp.stack([my_x, my_zl, my_y, my_core]).astype(jnp.int32)
    other_place = jnp.stack([my_x, my_zl, my_y, 1 - my_core]).astype(jnp.int32)
    one, two, rows, place, other_place, penalty = lax.optimization_barrier(
        (one, two, rows, place, other_place, penalty)
    )
    near = jnp.stack(
        gather_shifts(one, "col", shift_y, Y) + gather_shifts(two, "row", shift_x, X)
    )
    far = lax.ppermute(near, "col", shift_core(1))

    weights = (query_weight, key_weight, value_weight, gate_weight, output_weight)
    mine = attention(rows, weights, near, place, chain_weight, chain_ids, penalty)
    far, _ = lax.optimization_barrier((far, mine))
    update = attention(rows, weights, far, other_place, chain_weight, chain_ids, penalty, mine)
    held = lax.all_to_all(update, "row", split_axis=0, concat_axis=0, tiled=True).reshape(
        tile_cols, RATIO, tile_cols, channels
    )
    held = jnp.transpose(held, (1, 0, 2, 3))
    other = [
        to_mirror(lax.dynamic_index_in_dim(held, (col + step) % RATIO, 0, keepdims=False), step, 0)
        for step in range(RATIO)
    ]
    back = [held[0]] + [lax.ppermute(held[m], "row", shift_x(-m)) for m in range(1, RATIO)]
    back = jnp.stack(back, axis=1).reshape(tile_cols, tile_rows, channels)
    base = jnp.transpose(2.0 * carried + back.astype(jnp.float32), (1, 0, 2))
    other = in_order(other, col % RATIO).reshape(tile_rows, tile_cols, channels)
    return (base + other.astype(jnp.float32)).astype(jnp.bfloat16)


def solution(mesh):
    placed = (P("row", "col", None),) + (P(),) * 13
    return jax.shard_map(
        per_device, mesh=mesh, in_specs=placed, out_specs=P("row", "col", None), check_vma=False
    )
```

```python
import math

import jax
import jax.numpy as jnp
from jax import lax
from jax.experimental import pallas as pl
from jax.experimental.pallas import tpu as pltpu
from jax.sharding import PartitionSpec as P

mask_penalty = 1000000000.0
norm_epsilon = 1e-05

X, ZH, ZL, Y, CORE = 4, 2, 4, 4, 2
ROWS, COLS = X * ZH, ZL * Y * CORE
RATIO = COLS // ROWS


def normalize(values, gain):
    center = values - jnp.mean(values, axis=-1, keepdims=True)
    variance = jnp.mean(center * center, axis=-1, keepdims=True)
    return center * lax.rsqrt(variance + norm_epsilon) * gain


def place_of(device):
    row, col = divmod(device, COLS)
    return row // ZH, row % ZH, col // (Y * CORE), col // CORE % Y, col % CORE


def device_of(x, zh, zl, y, core):
    return (x * ZH + zh) * COLS + (zl * Y + y) * CORE + core


def via(device, block, back=1, y_step=Y // 2):
    x, zh, zl, y, core = place_of(device)
    return device_of(
        (x + back * block) % X, zh, zl, (y + back * y_step * (block % 2)) % Y, core
    )


def out_pairs(block):
    return [(d, via(d, block)) for d in range(ROWS * COLS)]


def mirror_pairs(step, y_step):
    pairs = []
    for d in range(ROWS * COLS):
        block = (d + step) % RATIO
        row, col = divmod(via(d, block, -1, y_step), COLS)
        pairs.append((d, (col // RATIO) * COLS + RATIO * row + block))
    return pairs


def spread(blocks):
    return [blocks[0]] + [
        lax.ppermute(blocks[m], ("row", "col"), out_pairs(m)) for m in range(1, RATIO)
    ]


def to_mirror(piece, step, y_step):
    return lax.ppermute(piece, ("row", "col"), mirror_pairs(step, y_step))


def shift_x(k):
    return [(r, ((r // ZH + k) % X) * ZH + r % ZH) for r in range(ROWS)]


def shift_zh(k):
    return [(r, (r // ZH) * ZH + (r + k) % ZH) for r in range(ROWS)]


def shift_zl(k):
    return [(c, (c + k * Y * CORE) % COLS) for c in range(COLS)]


def shift_y(k):
    return [
        (c, c - c % (Y * CORE) + (c + k * CORE) % (Y * CORE)) for c in range(COLS)
    ]


def shift_core(k):
    return [(c, c ^ k) for c in range(COLS)]


def gather_shifts(array, axis, pairs, count):
    return [array] + [lax.ppermute(array, axis, pairs(k)) for k in range(1, count)]


def in_order(pieces, me):
    count = len(pieces)
    twice = jnp.stack(pieces[::-1] + pieces[::-1])
    return lax.dynamic_slice_in_dim(twice, count - 1 - me, count, 0)


def transition_kernel(
    col_ref, own_ref, got0, got1, got2, got3, gain1_ref, w1_ref, w2_ref, gain2_ref, wb_ref,
    carried_ref, normed_ref, bias_ref,
):
    col = col_ref[0]
    tile_cols, tile_rows, channels = own_ref.shape
    width = tile_rows // RATIO
    for step, got in enumerate((got0, got1, got2, got3)):
        start = pl.multiple_of(lax.rem(col + RATIO - step, RATIO) * width, width)
        own = own_ref[:, pl.ds(start, width), :].astype(jnp.float32)
        sym = (own + got[...].astype(jnp.float32)).reshape(tile_cols * width, channels)
        first = normalize(sym, gain1_ref[...]).astype(jnp.bfloat16)
        hidden = jnp.maximum(
            jnp.dot(first, w1_ref[...], preferred_element_type=jnp.float32), 0.0
        ).astype(jnp.bfloat16)
        carried = sym + jnp.dot(hidden, w2_ref[...], preferred_element_type=jnp.float32)
        normed = normalize(carried, gain2_ref[...]).astype(jnp.bfloat16)
        carried_ref[:, pl.ds(start, width), :] = carried.reshape(tile_cols, width, channels)
        normed_ref[:, pl.ds(start, width), :] = normed.reshape(tile_cols, width, channels)
    for b in range(tile_cols):
        bias_ref[b] = lax.dot_general(
            wb_ref[...], normed_ref[b], (((1,), (1,)), ((), ())),
            preferred_element_type=jnp.float32,
        ).astype(jnp.bfloat16)


def transition(own, got, col, gain1, w1, w2, gain2, wb):
    tile_cols, tile_rows, channels = own.shape
    heads = wb.shape[1]
    vmem = pl.BlockSpec(memory_space=pltpu.VMEM)
    return pl.pallas_call(
        transition_kernel,
        out_shape=(
            jax.ShapeDtypeStruct(own.shape, jnp.float32),
            jax.ShapeDtypeStruct(own.shape, jnp.bfloat16),
            jax.ShapeDtypeStruct((tile_cols, heads, tile_rows), jnp.bfloat16),
        ),
        in_specs=[pl.BlockSpec(memory_space=pltpu.SMEM)] + [vmem] * 10,
        out_specs=(vmem, vmem, vmem),
        compiler_params=pltpu.CompilerParams(vmem_limit_bytes=24 << 20),
        name="transition",
    )(col, own, *got, gain1[None], w1, w2, gain2[None], wb.T)


def attention_kernel(
    place_ref, cw_ref, rows_ref, wq_ref, wk_ref, wv_ref, wg_ref, wo_ref, a_ref, b_ref,
    chain_col_ref, chain_row_ref, penalty_ref, *refs,
):
    begun_refs, (out_ref, kt_ref, v_ref) = refs[:-3], refs[-3:]
    my_x, my_zl, my_y, core = place_ref[0], place_ref[1], place_ref[2], place_ref[3]
    parts, own_rows, part_len, channels = rows_ref.shape
    z_steps, half, strip = a_ref.shape[1], a_ref.shape[3], a_ref.shape[4]
    heads = 2 * half
    head_dim = channels // heads
    scale = 1.0 / math.sqrt(head_dim)
    xs = [lax.rem(my_x + X - step, X) for step in range(X)]

    @pl.when(pl.program_id(0) == 0)
    def _():
        for begun_ref in begun_refs:
            out_ref[...] = begun_ref[...]
        for i in range(own_rows):
            row = jnp.concatenate([rows_ref[x * ZH + zh, i] for x in xs for zh in range(ZH)])
            kt_ref[i] = lax.dot_general(
                wk_ref[...], row, (((0,), (1,)), ((), ())), preferred_element_type=jnp.float32
            ).astype(jnp.bfloat16)
            v_ref[i] = jnp.dot(
                row, wv_ref[...], preferred_element_type=jnp.float32
            ).astype(jnp.bfloat16)

    per_part = part_len // strip
    places = []
    for z in range(z_steps):
        zl = lax.rem(my_zl + ZL - (pl.program_id(0) * z_steps + z), ZL)
        for y_step in range(Y):
            within = lax.rem(my_y + Y - y_step, Y) * CORE + core
            part = zl * (Y * CORE // per_part) + within // per_part
            places.append((part, lax.rem(within, per_part)))
    starts = [pl.multiple_of(block * strip, strip) for _, block in places]
    chain_rows = jnp.concatenate(
        [
            chain_col_ref[pl.ds(pl.multiple_of(part * part_len, part_len) + start, strip), :]
            for (part, _), start in zip(places, starts)
        ]
    )
    chain_keys = jnp.concatenate([chain_row_ref[pl.ds(x, 1), :] for x in xs], axis=1)
    penalty = jnp.concatenate([penalty_ref[pl.ds(x, 1), :] for x in xs], axis=1)
    same = (chain_rows == chain_keys).astype(jnp.float32)
    lane_head = lax.broadcasted_iota(jnp.int32, (1, channels), 1) // head_dim
    queries, gates, mixes = [], [], []
    for i in range(own_rows):
        part_rows = jnp.concatenate(
            [rows_ref[part, i, pl.ds(start, strip), :] for (part, _), start in zip(places, starts)]
        )
        queries.append(
            jnp.dot(part_rows, wq_ref[...], preferred_element_type=jnp.float32).astype(jnp.bfloat16)
        )
        gates.append(
            jax.nn.sigmoid(jnp.dot(part_rows, wg_ref[...], preferred_element_type=jnp.float32))
        )
        mixes.append(jnp.zeros((len(places) * strip, channels), jnp.float32))
    count = len(places) * strip
    masked = [lane_head == h for h in range(heads)]
    products = [
        jnp.dot(
            jnp.concatenate(
                [jnp.where(mine, query, jnp.zeros_like(query)) for mine in masked]
            ),
            kt_ref[i],
            preferred_element_type=jnp.float32,
        )
        for i, query in enumerate(queries)
    ]
    weights = [[] for _ in range(own_rows)]
    for h in range(heads):
        strips = []
        for z in range(z_steps):
            for y_step in range(Y):
                if h < half:
                    chunks = [a_ref[y_step, z, k, h] for k in range(X)]
                else:
                    chunks = [b_ref[k, y_step, z, h - half] for k in range(X)]
                strips.append(jnp.concatenate(chunks, axis=1))
        pair = jnp.concatenate(strips).astype(jnp.float32)
        full = pair + cw_ref[h] * same - penalty
        for i in range(own_rows):
            scores = products[i][h * count : (h + 1) * count] * scale + full
            exponent = jnp.exp(scores - jnp.max(scores, axis=-1, keepdims=True))
            weights[i].append(
                (exponent * (1.0 / jnp.sum(exponent, axis=-1, keepdims=True))).astype(
                    jnp.bfloat16
                )
            )
    for i in range(own_rows):
        mixed = jnp.dot(
            jnp.concatenate(weights[i]), v_ref[i], preferred_element_type=jnp.float32
        )
        for h, mine in enumerate(masked):
            mixes[i] = jnp.where(mine, mixed[h * count : (h + 1) * count], mixes[i])
    for i in range(own_rows):
        gated = (gates[i] * mixes[i]).astype(jnp.bfloat16)
        update = jnp.dot(gated, wo_ref[...], preferred_element_type=jnp.float32).astype(
            jnp.bfloat16
        )
        for n, (part, block) in enumerate(places):
            to = lax.rem(part // ZH + block, X) * ZH + lax.rem(part, ZH)
            out_ref[to, i, block] = update[n * strip : (n + 1) * strip]


def attention(rows, weights, bias, place, chain_weight, chain_ids, penalty, begun=None):
    parts, own_rows, part_len, channels = rows.shape
    half, strip, width = bias.shape[3:]
    length = parts * part_len
    z_steps = ZL
    smem = pl.BlockSpec(memory_space=pltpu.SMEM)

    def whole(shape):
        return pl.BlockSpec(shape, lambda g: (0,) * len(shape))

    first = pl.BlockSpec((Y, z_steps, X, half, strip, width), lambda g: (0, g, 0, 0, 0, 0))
    second = pl.BlockSpec((X, Y, z_steps, half, strip, width), lambda g: (1, 0, g, 0, 0, 0))
    out_shape = (parts, own_rows, part_len // strip, strip, channels)
    begun = [] if begun is None else [begun]
    scores = own_rows * length // CORE * length * 2 * half
    return pl.pallas_call(
        attention_kernel,
        out_shape=jax.ShapeDtypeStruct(out_shape, jnp.bfloat16),
        grid=(ZL // z_steps,),
        in_specs=[smem, smem, whole(rows.shape)]
        + [whole(w.shape) for w in weights]
        + [first, second, whole((length, 1)), whole((X, width)), whole((X, width))]
        + [whole(out_shape)] * len(begun),
        out_specs=whole(out_shape),
        scratch_shapes=[
            pltpu.VMEM((own_rows, channels, length), jnp.bfloat16),
            pltpu.VMEM((own_rows, length, channels), jnp.bfloat16),
        ],
        compiler_params=pltpu.CompilerParams(vmem_limit_bytes=28 << 20),
        cost_estimate=pl.CostEstimate(
            flops=4 * scores * channels,
            bytes_accessed=2 * scores // own_rows + 10 * own_rows * length * channels,
            transcendentals=scores,
        ),
        name="attention",
    )(
        place, chain_weight, rows, *weights, bias, bias, chain_ids[:, None],
        chain_ids.reshape(X, width), penalty.reshape(X, width), *begun,
    )


def per_device(
    pair_state,
    residue_mask,
    chain_ids,
    gain_transition,
    hidden_weight,
    out_weight,
    gain_attention,
    query_weight,
    key_weight,
    value_weight,
    gate_weight,
    bias_weight,
    chain_weight,
    output_weight,
):
    tile_rows, tile_cols, channels = pair_state.shape
    heads = chain_weight.shape[0]
    row, col = lax.axis_index("row"), lax.axis_index("col")
    my_x, my_zh = row // ZH, row % ZH
    my_zl, my_y, my_core = col // (Y * CORE), col // CORE % Y, col % CORE

    blocks = pair_state.reshape(RATIO, tile_cols, tile_cols, channels)
    held = jnp.stack(spread(blocks))
    got = [
        to_mirror(
            lax.dynamic_index_in_dim(held, (col + step) % RATIO, 0, keepdims=False), step, Y // 2
        )
        for step in range(RATIO)
    ]
    own = jnp.transpose(pair_state, (1, 0, 2))
    carried, normed, bias = transition(
        own, got, col.reshape(1), gain_transition, hidden_weight, out_weight, gain_attention,
        bias_weight,
    )

    by_zh = in_order(gather_shifts(bias, "row", shift_zh, ZH), my_zh)
    chunk = jnp.transpose(by_zh, (2, 1, 0, 3)).reshape(heads, tile_cols, ZH * tile_rows)
    one, two = chunk[: heads // 2], chunk[heads // 2 :]
    one = jnp.stack(gather_shifts(one, "row", shift_x, X))
    two = jnp.stack(gather_shifts(two, "col", shift_zl, ZL))

    sent = normed.reshape(ROWS, tile_cols // ROWS, tile_rows, channels)
    sent, _ = lax.optimization_barrier((sent, by_zh))
    rows = lax.all_to_all(sent, "row", split_axis=0, concat_axis=0, tiled=True)

    one = jnp.stack(gather_shifts(one, "col", shift_zl, ZL))
    two = jnp.stack(gather_shifts(two, "col", shift_y, Y))
    penalty = mask_penalty * (1 - residue_mask).astype(jnp.float32)
    place = jnp.stack([my_x, my_zl, my_y, my_core]).astype(jnp.int32)
    other_place = jnp.stack([my_x, my_zl, my_y, 1 - my_core]).astype(jnp.int32)
    one, two, rows, place, other_place, penalty = lax.optimization_barrier(
        (one, two, rows, place, other_place, penalty)
    )
    near = jnp.stack(
        gather_shifts(one, "col", shift_y, Y) + gather_shifts(two, "row", shift_x, X)
    )
    far = lax.ppermute(near, "col", shift_core(1))

    weights = (query_weight, key_weight, value_weight, gate_weight, output_weight)
    mine = attention(rows, weights, near, place, chain_weight, chain_ids, penalty)
    far, _ = lax.optimization_barrier((far, mine))
    update = attention(rows, weights, far, other_place, chain_weight, chain_ids, penalty, mine)
    held = lax.all_to_all(update, "row", split_axis=0, concat_axis=0, tiled=True).reshape(
        tile_cols, RATIO, tile_cols, channels
    )
    held = jnp.transpose(held, (1, 0, 2, 3))
    other = [
        to_mirror(lax.dynamic_index_in_dim(held, (col + step) % RATIO, 0, keepdims=False), step, 0)
        for step in range(RATIO)
    ]
    back = [held[0]] + [lax.ppermute(held[m], "row", shift_x(-m)) for m in range(1, RATIO)]
    back = jnp.stack(back, axis=1).reshape(tile_cols, tile_rows, channels)
    base = jnp.transpose(2.0 * carried + back.astype(jnp.float32), (1, 0, 2))
    other = in_order(other, col % RATIO).reshape(tile_rows, tile_cols, channels)
    return (base + other.astype(jnp.float32)).astype(jnp.bfloat16)


def solution(mesh):
    placed = (P("row", "col", None),) + (P(),) * 13
    return jax.shard_map(
        per_device, mesh=mesh, in_specs=placed, out_specs=P("row", "col", None), check_vma=False
    )
```

```python
import math

import jax
import jax.numpy as jnp
from jax import lax
from jax.experimental import pallas as pl
from jax.experimental.pallas import tpu as pltpu
from jax.sharding import PartitionSpec as P

mask_penalty = 1000000000.0
norm_epsilon = 1e-05

X, ZH, ZL, Y, CORE = 4, 2, 4, 4, 2
ROWS, COLS = X * ZH, ZL * Y * CORE
RATIO = COLS // ROWS


def normalize(values, gain):
    center = values - jnp.mean(values, axis=-1, keepdims=True)
    variance = jnp.mean(center * center, axis=-1, keepdims=True)
    return center * lax.rsqrt(variance + norm_epsilon) * gain


def place_of(device):
    row, col = divmod(device, COLS)
    return row // ZH, row % ZH, col // (Y * CORE), col // CORE % Y, col % CORE


def device_of(x, zh, zl, y, core):
    return (x * ZH + zh) * COLS + (zl * Y + y) * CORE + core


def via(device, block, back=1, y_step=Y // 2):
    x, zh, zl, y, core = place_of(device)
    return device_of(
        (x + back * block) % X, zh, zl, (y + back * y_step * (block % 2)) % Y, core
    )


def out_pairs(block):
    return [(d, via(d, block)) for d in range(ROWS * COLS)]


def mirror_pairs(step, y_step):
    pairs = []
    for d in range(ROWS * COLS):
        block = (d + step) % RATIO
        row, col = divmod(via(d, block, -1, y_step), COLS)
        pairs.append((d, (col // RATIO) * COLS + RATIO * row + block))
    return pairs


def spread(blocks):
    return [blocks[0]] + [
        lax.ppermute(blocks[m], ("row", "col"), out_pairs(m)) for m in range(1, RATIO)
    ]


def to_mirror(piece, step, y_step):
    return lax.ppermute(piece, ("row", "col"), mirror_pairs(step, y_step))


def shift_x(k):
    return [(r, ((r // ZH + k) % X) * ZH + r % ZH) for r in range(ROWS)]


def shift_zh(k):
    return [(r, (r // ZH) * ZH + (r + k) % ZH) for r in range(ROWS)]


def shift_zl(k):
    return [(c, (c + k * Y * CORE) % COLS) for c in range(COLS)]


def shift_y(k):
    return [
        (c, c - c % (Y * CORE) + (c + k * CORE) % (Y * CORE)) for c in range(COLS)
    ]


def shift_core(k):
    return [(c, c ^ k) for c in range(COLS)]


def gather_shifts(array, axis, pairs, count):
    return [array] + [lax.ppermute(array, axis, pairs(k)) for k in range(1, count)]


def in_order(pieces, me):
    count = len(pieces)
    twice = jnp.stack(pieces[::-1] + pieces[::-1])
    return lax.dynamic_slice_in_dim(twice, count - 1 - me, count, 0)


def transition_kernel(
    col_ref, own_ref, got0, got1, got2, got3, gain1_ref, w1_ref, w2_ref, gain2_ref, wb_ref,
    carried_ref, normed_ref, bias_ref,
):
    col = col_ref[0]
    tile_cols, tile_rows, channels = own_ref.shape
    width = tile_rows // RATIO
    for step, got in enumerate((got0, got1, got2, got3)):
        start = pl.multiple_of(lax.rem(col + RATIO - step, RATIO) * width, width)
        own = own_ref[:, pl.ds(start, width), :].astype(jnp.float32)
        sym = (own + got[...].astype(jnp.float32)).reshape(tile_cols * width, channels)
        first = normalize(sym, gain1_ref[...]).astype(jnp.bfloat16)
        hidden = jnp.maximum(
            jnp.dot(first, w1_ref[...], preferred_element_type=jnp.float32), 0.0
        ).astype(jnp.bfloat16)
        carried = sym + jnp.dot(hidden, w2_ref[...], preferred_element_type=jnp.float32)
        normed = normalize(carried, gain2_ref[...]).astype(jnp.bfloat16)
        carried_ref[:, pl.ds(start, width), :] = carried.reshape(tile_cols, width, channels)
        normed_ref[:, pl.ds(start, width), :] = normed.reshape(tile_cols, width, channels)
    for b in range(tile_cols):
        bias_ref[b] = lax.dot_general(
            wb_ref[...], normed_ref[b], (((1,), (1,)), ((), ())),
            preferred_element_type=jnp.float32,
        ).astype(jnp.bfloat16)


def transition(own, got, col, gain1, w1, w2, gain2, wb):
    tile_cols, tile_rows, channels = own.shape
    heads = wb.shape[1]
    vmem = pl.BlockSpec(memory_space=pltpu.VMEM)
    return pl.pallas_call(
        transition_kernel,
        out_shape=(
            jax.ShapeDtypeStruct(own.shape, jnp.float32),
            jax.ShapeDtypeStruct(own.shape, jnp.bfloat16),
            jax.ShapeDtypeStruct((tile_cols, heads, tile_rows), jnp.bfloat16),
        ),
        in_specs=[pl.BlockSpec(memory_space=pltpu.SMEM)] + [vmem] * 10,
        out_specs=(vmem, vmem, vmem),
        compiler_params=pltpu.CompilerParams(vmem_limit_bytes=24 << 20),
        name="transition",
    )(col, own, *got, gain1[None], w1, w2, gain2[None], wb.T)


def attention_kernel(
    place_ref, cw_ref, rows_ref, wq_ref, wk_ref, wv_ref, wg_ref, wo_ref, a_ref, b_ref,
    chain_col_ref, chain_row_ref, penalty_ref, *refs,
):
    begun_refs, (out_ref, kt_ref, v_ref) = refs[:-3], refs[-3:]
    my_x, my_zl, my_y, core = place_ref[0], place_ref[1], place_ref[2], place_ref[3]
    parts, own_rows, part_len, channels = rows_ref.shape
    z_steps, half, strip = a_ref.shape[1], a_ref.shape[3], a_ref.shape[4]
    heads = 2 * half
    head_dim = channels // heads
    scale = 1.0 / math.sqrt(head_dim)
    xs = [lax.rem(my_x + X - step, X) for step in range(X)]

    @pl.when(pl.program_id(0) == 0)
    def _():
        for begun_ref in begun_refs:
            out_ref[...] = begun_ref[...]
        for i in range(own_rows):
            row = jnp.concatenate([rows_ref[x * ZH + zh, i] for x in xs for zh in range(ZH)])
            kt_ref[i] = lax.dot_general(
                wk_ref[...], row, (((0,), (1,)), ((), ())), preferred_element_type=jnp.float32
            ).astype(jnp.bfloat16)
            v_ref[i] = jnp.dot(
                row, wv_ref[...], preferred_element_type=jnp.float32
            ).astype(jnp.bfloat16)

    per_part = part_len // strip
    places = []
    for z in range(z_steps):
        zl = lax.rem(my_zl + ZL - (pl.program_id(0) * z_steps + z), ZL)
        for y_step in range(Y):
            within = lax.rem(my_y + Y - y_step, Y) * CORE + core
            part = zl * (Y * CORE // per_part) + within // per_part
            places.append((part, lax.rem(within, per_part)))
    starts = [pl.multiple_of(block * strip, strip) for _, block in places]
    chain_rows = jnp.concatenate(
        [
            chain_col_ref[pl.ds(pl.multiple_of(part * part_len, part_len) + start, strip), :]
            for (part, _), start in zip(places, starts)
        ]
    )
    chain_keys = jnp.concatenate([chain_row_ref[pl.ds(x, 1), :] for x in xs], axis=1)
    penalty = jnp.concatenate([penalty_ref[pl.ds(x, 1), :] for x in xs], axis=1)
    same = (chain_rows == chain_keys).astype(jnp.float32)
    lane_head = lax.broadcasted_iota(jnp.int32, (1, channels), 1) // head_dim
    queries, gates, mixes = [], [], []
    for i in range(own_rows):
        part_rows = jnp.concatenate(
            [rows_ref[part, i, pl.ds(start, strip), :] for (part, _), start in zip(places, starts)]
        )
        queries.append(
            jnp.dot(part_rows, wq_ref[...], preferred_element_type=jnp.float32).astype(jnp.bfloat16)
        )
        gates.append(
            jax.nn.sigmoid(jnp.dot(part_rows, wg_ref[...], preferred_element_type=jnp.float32))
        )
        mixes.append(jnp.zeros((len(places) * strip, channels), jnp.float32))
    count = len(places) * strip
    masked = [lane_head == h for h in range(heads)]
    products = [
        jnp.dot(
            jnp.concatenate(
                [jnp.where(mine, query, jnp.zeros_like(query)) for mine in masked]
            ),
            kt_ref[i],
            preferred_element_type=jnp.float32,
        )
        for i, query in enumerate(queries)
    ]
    weights = [[] for _ in range(own_rows)]
    for h in range(heads):
        strips = []
        for z in range(z_steps):
            for y_step in range(Y):
                if h < half:
                    chunks = [a_ref[y_step, z, k, h] for k in range(X)]
                else:
                    chunks = [b_ref[k, y_step, z, h - half] for k in range(X)]
                strips.append(jnp.concatenate(chunks, axis=1))
        pair = jnp.concatenate(strips).astype(jnp.float32)
        full = pair + cw_ref[h] * same - penalty
        for i in range(own_rows):
            scores = products[i][h * count : (h + 1) * count] * scale + full
            exponent = jnp.exp(scores - jnp.max(scores, axis=-1, keepdims=True))
            weights[i].append(
                (exponent * (1.0 / jnp.sum(exponent, axis=-1, keepdims=True))).astype(
                    jnp.bfloat16
                )
            )
    for i in range(own_rows):
        mixed = jnp.dot(
            jnp.concatenate(weights[i]), v_ref[i], preferred_element_type=jnp.float32
        )
        for h, mine in enumerate(masked):
            mixes[i] = jnp.where(mine, mixed[h * count : (h + 1) * count], mixes[i])
    for i in range(own_rows):
        gated = (gates[i] * mixes[i]).astype(jnp.bfloat16)
        update = jnp.dot(gated, wo_ref[...], preferred_element_type=jnp.float32).astype(
            jnp.bfloat16
        )
        for n, (part, block) in enumerate(places):
            to = lax.rem(part // ZH + block, X) * ZH + lax.rem(part, ZH)
            out_ref[to, i, block] = update[n * strip : (n + 1) * strip]


def attention(rows, weights, bias, place, chain_weight, chain_ids, penalty, begun=None):
    parts, own_rows, part_len, channels = rows.shape
    half, strip, width = bias.shape[3:]
    length = parts * part_len
    z_steps = ZL // 2
    smem = pl.BlockSpec(memory_space=pltpu.SMEM)

    def whole(shape):
        return pl.BlockSpec(shape, lambda g: (0,) * len(shape))

    first = pl.BlockSpec((Y, z_steps, X, half, strip, width), lambda g: (0, g, 0, 0, 0, 0))
    second = pl.BlockSpec((X, Y, z_steps, half, strip, width), lambda g: (1, 0, g, 0, 0, 0))
    out_shape = (parts, own_rows, part_len // strip, strip, channels)
    begun = [] if begun is None else [begun]
    scores = own_rows * length // CORE * length * 2 * half
    return pl.pallas_call(
        attention_kernel,
        out_shape=jax.ShapeDtypeStruct(out_shape, jnp.bfloat16),
        grid=(ZL // z_steps,),
        in_specs=[smem, smem, whole(rows.shape)]
        + [whole(w.shape) for w in weights]
        + [first, second, whole((length, 1)), whole((X, width)), whole((X, width))]
        + [whole(out_shape)] * len(begun),
        out_specs=whole(out_shape),
        scratch_shapes=[
            pltpu.VMEM((own_rows, channels, length), jnp.bfloat16),
            pltpu.VMEM((own_rows, length, channels), jnp.bfloat16),
        ],
        compiler_params=pltpu.CompilerParams(vmem_limit_bytes=20 << 20),
        cost_estimate=pl.CostEstimate(
            flops=4 * scores * channels,
            bytes_accessed=2 * scores // own_rows + 10 * own_rows * length * channels,
            transcendentals=scores,
        ),
        name="attention",
    )(
        place, chain_weight, rows, *weights, bias, bias, chain_ids[:, None],
        chain_ids.reshape(X, width), penalty.reshape(X, width), *begun,
    )


def per_device(
    pair_state,
    residue_mask,
    chain_ids,
    gain_transition,
    hidden_weight,
    out_weight,
    gain_attention,
    query_weight,
    key_weight,
    value_weight,
    gate_weight,
    bias_weight,
    chain_weight,
    output_weight,
):
    tile_rows, tile_cols, channels = pair_state.shape
    heads = chain_weight.shape[0]
    row, col = lax.axis_index("row"), lax.axis_index("col")
    my_x, my_zh = row // ZH, row % ZH
    my_zl, my_y, my_core = col // (Y * CORE), col // CORE % Y, col % CORE

    blocks = pair_state.reshape(RATIO, tile_cols, tile_cols, channels)
    held = jnp.stack(spread(blocks))
    got = [
        to_mirror(
            lax.dynamic_index_in_dim(held, (col + step) % RATIO, 0, keepdims=False), step, Y // 2
        )
        for step in range(RATIO)
    ]
    own = jnp.transpose(pair_state, (1, 0, 2))
    carried, normed, bias = transition(
        own, got, col.reshape(1), gain_transition, hidden_weight, out_weight, gain_attention,
        bias_weight,
    )

    by_zh = in_order(gather_shifts(bias, "row", shift_zh, ZH), my_zh)
    chunk = jnp.transpose(by_zh, (2, 1, 0, 3)).reshape(heads, tile_cols, ZH * tile_rows)
    one, two = chunk[: heads // 2], chunk[heads // 2 :]
    one = jnp.stack(gather_shifts(one, "row", shift_x, X))
    two = jnp.stack(gather_shifts(two, "col", shift_zl, ZL))

    sent = normed.reshape(ROWS, tile_cols // ROWS, tile_rows, channels)
    sent, _ = lax.optimization_barrier((sent, by_zh))
    rows = lax.all_to_all(sent, "row", split_axis=0, concat_axis=0, tiled=True)

    one = jnp.stack(gather_shifts(one, "col", shift_zl, ZL))
    two = jnp.stack(gather_shifts(two, "col", shift_y, Y))
    penalty = mask_penalty * (1 - residue_mask).astype(jnp.float32)
    place = jnp.stack([my_x, my_zl, my_y, my_core]).astype(jnp.int32)
    other_place = jnp.stack([my_x, my_zl, my_y, 1 - my_core]).astype(jnp.int32)
    one, two, rows, place, other_place, penalty = lax.optimization_barrier(
        (one, two, rows, place, other_place, penalty)
    )
    near = jnp.stack(
        gather_shifts(one, "col", shift_y, Y) + gather_shifts(two, "row", shift_x, X)
    )
    far = lax.ppermute(near, "col", shift_core(1))

    weights = (query_weight, key_weight, value_weight, gate_weight, output_weight)
    mine = attention(rows, weights, near, place, chain_weight, chain_ids, penalty)
    far, _ = lax.optimization_barrier((far, mine))
    update = attention(rows, weights, far, other_place, chain_weight, chain_ids, penalty, mine)
    held = lax.all_to_all(update, "row", split_axis=0, concat_axis=0, tiled=True).reshape(
        tile_cols, RATIO, tile_cols, channels
    )
    held = jnp.transpose(held, (1, 0, 2, 3))
    other = [
        to_mirror(lax.dynamic_index_in_dim(held, (col + step) % RATIO, 0, keepdims=False), step, 0)
        for step in range(RATIO)
    ]
    back = [held[0]] + [lax.ppermute(held[m], "row", shift_x(-m)) for m in range(1, RATIO)]
    back = jnp.stack(back, axis=1).reshape(tile_cols, tile_rows, channels)
    base = jnp.transpose(2.0 * carried + back.astype(jnp.float32), (1, 0, 2))
    other = in_order(other, col % RATIO).reshape(tile_rows, tile_cols, channels)
    return (base + other.astype(jnp.float32)).astype(jnp.bfloat16)


def solution(mesh):
    placed = (P("row", "col", None),) + (P(),) * 13
    return jax.shard_map(
        per_device, mesh=mesh, in_specs=placed, out_specs=P("row", "col", None), check_vma=False
    )
```
